128 devices in a mesh: grp: 2 (over y_hi), seq: 64 (over y_lo, x, z, core).
Axes of the slice: x: 4, y: 4 (y_hi: 2, y_lo: 2; y = y_hi * 2 + y_lo), z: 4, core: 2. Of those that a mesh axis runs over, the one named last changes fastest.
Arguments:
- tokens: bfloat16 [16384, 2048], P(('grp', 'seq')), may hold values from -6 to 6
- lengths: int32 [2, 9], P('grp'), may hold values from 2 to 8124, as said below
- norm_gain: bfloat16 [2048], P('seq'), may hold values from 0.099609375 to 1.8984375
- w_query: bfloat16 [2048, 2048], P('seq'), may hold values from -0.125 to 0.125
- w_key: bfloat16 [2048, 2048], P('seq'), may hold values from -0.125 to 0.125
- w_value: bfloat16 [2048, 2048], P('seq'), may hold values from -0.125 to 0.125
- w_out: bfloat16 [2048, 2048], P('seq'), may hold values from -0.375 to 0.375
- mlp_gain: bfloat16 [2048], P('seq'), may hold values from 0.099609375 to 1.8984375
- w_gate: bfloat16 [2048, 5504], P('seq'), may hold values from -0.125 to 0.125
- w_up: bfloat16 [2048, 5504], P('seq'), may hold values from -0.125 to 0.125
- w_down: bfloat16 [5504, 2048], P('seq'), may hold values from -0.078125 to 0.078125
- cotangent: bfloat16 [16384, 2048], P(('grp', 'seq')), may hold values from -6 to 6
Outputs:
- outputs: bfloat16 [16384, 2048], P(('grp', 'seq'))
- input_grad: float32 [16384, 2048], P(('grp', 'seq'))
- gain_grad: float32 [2048], P('seq')
- query_grad: float32 [2048, 2048], P('seq')
- key_grad: float32 [2048, 2048], P('seq')
- value_grad: float32 [2048, 2048], P('seq')
- out_grad: float32 [2048, 2048], P('seq')
- mlp_gain_grad: float32 [2048], P('seq')
- gate_grad: float32 [2048, 5504], P('seq')
- up_grad: float32 [2048, 5504], P('seq')
- down_grad: float32 [5504, 2048], P('seq')
The draws below stay inside these ranges and needn't reach their ends.
Inputs may be any that keep to these rules, and one draw needn't show every extreme that they name: Each group's 9 lengths sum to 8192; exactly one of them is longer than 128, and that row starts among the first 128 positions and ends among the last 128; each other row has fewer than 16 tokens.
All inputs are finite; a program needn't handle non-finite values.
Results may differ from the reference program's by a relative error of at most 0.017.
Values may be sent and summed in bfloat16 or wider, within the bound.
No kernel may reach another device: no remote copies, remote signals or barrier semaphores. Data moves between devices by JAX's collectives and lax.ppermute only.
A program may use at most 640 MiB of HBM per device.

```python
from functools import partial
from functools import reduce
import jax
import jax.numpy as jnp
from jax import lax

D = 2048
FF = 5504
HEADS = 16
HEAD = 128
WIN = 64
NDOCS = 9
TOK_DEV = 128
STREAM = 8192
TOKENS = 16384
N_GRP = 2


def draw_lengths(key, part):
    key = jax.random.fold_in(key, 7)
    short_key, place_key = jax.random.split(key)
    pair_count = (NDOCS - 1) // 2
    pair_total = TOK_DEV // 8 + 1
    firsts = jax.random.randint(short_key, (N_GRP, pair_count), 2, TOK_DEV // 8, dtype=jnp.int32)
    pair_index = jnp.arange(pair_count, dtype=jnp.int32)[None, :]
    firsts = jnp.where(pair_index == 0, 2, firsts).astype(jnp.int32)
    seconds = (pair_total - firsts).astype(jnp.int32)
    shorts = jnp.stack([firsts, seconds], axis=2).reshape(N_GRP, NDOCS - 1).astype(jnp.int32)
    before = jax.random.randint(place_key, (N_GRP, 1), 0, NDOCS, dtype=jnp.int32)
    longest = STREAM - jnp.sum(shorts, axis=1, keepdims=True).astype(jnp.int32)
    zero_column = jnp.zeros((N_GRP, 1), jnp.int32)
    left_side = jnp.concatenate([shorts, zero_column], axis=1)
    right_side = jnp.concatenate([zero_column, shorts], axis=1)
    columns = jnp.arange(NDOCS, dtype=jnp.int32)[None, :]
    return jnp.where(columns < before, left_side, jnp.where(columns == before, longest, right_side)).astype(jnp.int32)


def block_levels(key, extent, cuts, least, high):
    factor_of = 1.0
    for position, blocks in cuts:
        heights = jax.random.uniform(jax.random.fold_in(jax.random.fold_in(key, 6), position), (blocks,), jnp.float32, least / len(cuts), high / len(cuts))
        factor_of = factor_of * jnp.repeat(jnp.exp(heights), extent[position] // blocks).reshape((-1,) + (1,) * (len(extent) - 1 - position))
    return factor_of


def scatter_about(rng, shape, deviation, most, pieces=(), held_as=jnp.bfloat16):
    factor_of = block_levels(rng, shape, pieces, -0.22, 0.18) if pieces else 1.0
    array = jax.random.normal(rng, shape, jnp.float32) * deviation * factor_of
    return jnp.minimum(jnp.maximum(array, -most), most).astype(held_as)


def setup_inputs(seed: int = 0) -> dict:
    arg_keys = jax.random.split(jax.random.key(seed), 13)
    tokens = scatter_about(arg_keys[0], (TOKENS, D), 1.0, 6.0, ((0, 128),))
    lengths = draw_lengths(jax.random.fold_in(arg_keys[12], 71), 0)
    norm_gain = jnp.clip(1.0 + 0.18 * jax.random.normal(arg_keys[2], (D,), jnp.float32), 0.099609375, 1.8984375).astype(jnp.bfloat16)
    w_query = scatter_about(arg_keys[3], (D, D), D ** -0.5, 0.125, ((0, 64),))
    w_key = scatter_about(arg_keys[4], (D, D), D ** -0.5, 0.125, ((0, 64),))
    w_value = scatter_about(arg_keys[5], (D, D), D ** -0.5, 0.125, ((0, 64),))
    w_out = scatter_about(arg_keys[6], (D, D), (D // 8) ** -0.5, 0.375, ((0, 64),))
    mlp_gain = jnp.clip(1.0 + 0.18 * jax.random.normal(arg_keys[7], (D,), jnp.float32), 0.099609375, 1.8984375).astype(jnp.bfloat16)
    w_gate = scatter_about(arg_keys[8], (D, FF), D ** -0.5, 0.125, ((0, 64),))
    w_up = scatter_about(arg_keys[9], (D, FF), D ** -0.5, 0.125, ((0, 64),))
    w_down = scatter_about(arg_keys[10], (FF, D), FF ** -0.5, 0.078125, ((0, 64),))
    cotangent = scatter_about(arg_keys[11], (TOKENS, D), 1.0, 6.0, ((0, 128),))
    return {"tokens": tokens, "lengths": lengths, "norm_gain": norm_gain, "w_query": w_query, "w_key": w_key, "w_value": w_value, "w_out": w_out, "mlp_gain": mlp_gain, "w_gate": w_gate, "w_up": w_up, "w_down": w_down, "cotangent": cotangent}


epsilon = 1e-06
block_rows = 512

@jax.custom_vjp
def low(v):
    return lax.optimization_barrier(v.astype(jnp.bfloat16)).astype(jnp.float32)

@jax.custom_vjp
def low_back(v):
    return v

def low_keep(v):
    return (low(v), None)

def low_pass(kept, grad):
    return (grad,)

def back_keep(v):
    return (v, None)

def back_low(kept, grad):
    return (low(grad),)
low.defvjp(low_keep, low_pass)
low_back.defvjp(back_keep, back_low)

def exact_dot(left, right):
    return jnp.dot(left, right, precision=lax.Precision.HIGHEST, preferred_element_type=jnp.float32)

def segment_numbers(positions, lengths):
    row_ends = jnp.cumsum(lengths).astype(jnp.int32)
    return lax.optimization_barrier(jnp.sum((positions[:, None] >= row_ends[None, :]).astype(jnp.int32), axis=1)).astype(jnp.int32)

def inverse_rms(values):
    return lax.rsqrt(lax.optimization_barrier(jnp.mean(values * values, axis=-1, keepdims=True)) + epsilon)

def stream_forward(lengths, inputs, norm_gain, w_query, w_key, w_value, w_out, mlp_gain, w_gate, w_up, w_down):
    stream_rows = inputs.shape[0]
    normed = low(inputs * inverse_rms(inputs) * norm_gain)
    queries = low(low_back(exact_dot(normed, w_query)))
    key_rows = low(low_back(exact_dot(normed, w_key)))
    value_rows = low(low_back(exact_dot(normed, w_value)))
    segments = segment_numbers(jnp.arange(stream_rows, dtype=jnp.int32), lengths)
    padded_keys = jnp.concatenate([jnp.zeros((WIN, D), jnp.float32), key_rows], axis=0)
    padded_values = jnp.concatenate([jnp.zeros((WIN, D), jnp.float32), value_rows], axis=0)
    padded_segments = jnp.concatenate([jnp.full((WIN,), -1, jnp.int32), segments], axis=0)
    offsets = jnp.arange(block_rows, dtype=jnp.int32)[:, None] - jnp.arange(block_rows + WIN, dtype=jnp.int32)[None, :] + WIN
    in_window = (offsets >= 0) & (offsets < WIN)

    def attend(block_index):
        first_row = (block_index * block_rows).astype(jnp.int32)
        block_queries = lax.dynamic_slice_in_dim(queries, first_row, block_rows, 0).reshape(block_rows, HEADS, HEAD)
        block_keys = lax.dynamic_slice_in_dim(padded_keys, first_row, block_rows + WIN, 0).reshape(block_rows + WIN, HEADS, HEAD)
        block_values = lax.dynamic_slice_in_dim(padded_values, first_row, block_rows + WIN, 0).reshape(block_rows + WIN, HEADS, HEAD)
        query_segments = lax.dynamic_slice_in_dim(segments, first_row, block_rows, 0)
        key_segments = lax.dynamic_slice_in_dim(padded_segments, first_row, block_rows + WIN, 0)
        allowed = in_window & (query_segments[:, None] == key_segments[None, :])
        scores = jnp.einsum('qhd,khd->hqk', block_queries, block_keys, precision=lax.Precision.HIGHEST)
        scores = low_back(scores * HEAD ** (-0.5))
        scores = jnp.where(allowed[None], scores, -1e+30)
        largest = lax.optimization_barrier(jnp.max(scores, axis=-1, keepdims=True))
        weights = jnp.exp(scores - largest)
        probabilities = weights / lax.optimization_barrier(jnp.sum(weights, axis=-1, keepdims=True))
        mixed_block = jnp.einsum('hqk,khd->qhd', low(probabilities), block_values, precision=lax.Precision.HIGHEST)
        return mixed_block.reshape(block_rows, D)
    block_indices = jnp.arange(stream_rows // block_rows, dtype=jnp.int32)
    mixed_heads = lax.map(jax.checkpoint(attend), block_indices).reshape(stream_rows, D)
    mixed_heads = low(low_back(mixed_heads))
    hidden_state = inputs + low_back(exact_dot(mixed_heads, w_out))
    normed_again = low(hidden_state * inverse_rms(hidden_state) * mlp_gain)
    gate_proj = low_back(exact_dot(normed_again, w_gate))
    up_proj = low_back(exact_dot(normed_again, w_up))
    activated = low(jax.nn.silu(gate_proj) * up_proj)
    return hidden_state + low_back(exact_dot(activated, w_down))

def reference(tokens, lengths, norm_gain, w_query, w_key, w_value, w_out, mlp_gain, w_gate, w_up, w_down, cotangent):
    params = [weight.astype(jnp.float32) for weight in (norm_gain, w_query, w_key, w_value, w_out, mlp_gain, w_gate, w_up, w_down)]
    output_list = []
    input_list = []
    group_grads = []
    for group in range(N_GRP):
        first_token = group * STREAM
        inputs = tokens[first_token:first_token + STREAM].astype(jnp.float32)
        upstream = cotangent[first_token:first_token + STREAM].astype(jnp.float32)
        result, pullback = jax.vjp(partial(stream_forward, lengths[group]), inputs, params[0], params[1], params[2], params[3], params[4], params[5], params[6], params[7], params[8])
        grads = pullback(upstream)
        output_list.append(result.astype(jnp.bfloat16))
        input_list.append(grads[0])
        group_grads.append(grads[1:])
    summed = [reduce(lambda left, right: left + right, [record[index_pos] for record in group_grads]) for index_pos in range(9)]
    return (jnp.concatenate(output_list, axis=0), jnp.concatenate(input_list, axis=0), summed[0], summed[1], summed[2], summed[3], summed[4], summed[5], summed[6], summed[7], summed[8])
```

```python
import functools

import jax
import jax.numpy as jnp
from jax import lax
from jax.experimental import pallas as pl
from jax.experimental.pallas import tpu as pltpu
from jax.sharding import Mesh
from jax.sharding import PartitionSpec as P

HEAD = 128
WIN = 64
BLOCK = 128
epsilon = 1e-06

TEAM = ("z", "c")
FLEET = ("yl", "x")
SEQ = ("yl", "x", "z", "c")
ALL = ("g", "yl", "x", "z", "c")
N_Z, N_C, N_TEAM, N_FLEET = 4, 2, 8, 8
SCALE = HEAD ** (-0.5)
low = jnp.bfloat16
full = jnp.float32


def from_ahead(value, axis, by):
    n = lax.axis_size(axis)
    return lax.ppermute(value, axis, [((i + by) % n, i) for i in range(n)])


def along_line(value, by):
    return lax.ppermute(
        value, FLEET, [(i, i + by) for i in range(N_FLEET) if 0 <= i + by < N_FLEET]
    )


def swapped(value):
    return lax.ppermute(
        value, SEQ, [(N_TEAM * f + t, N_TEAM * t + f) for f in range(N_FLEET) for t in range(N_TEAM)]
    )


def team_gather(value):
    mine = jnp.concatenate([value] + [from_ahead(value, "z", k) for k in range(1, N_Z)], axis=0)
    return jnp.concatenate([mine, from_ahead(mine, "c", 1)], axis=0)


def team_scatter(parts):
    rows = parts.shape[0] // N_TEAM
    half = N_Z * rows
    there = from_ahead(parts[half:].astype(low), "c", 1)
    pair = parts[:half].astype(full) + there.astype(full)
    total = pair[:rows]
    for k in range(1, N_Z):
        total = total + from_ahead(pair[k * rows : (k + 1) * rows].astype(low), "z", -k).astype(full)
    return total


def inverse_rms(values):
    return lax.rsqrt(jnp.mean(values * values, axis=-1, keepdims=True) + epsilon)


def matmul(left, right):
    return jnp.dot(left, right, preferred_element_type=full)


def matmul_left_t(left, right):
    return lax.dot_general(left, right, (((0,), (0,)), ((), ())), preferred_element_type=full)


def matmul_right_t(left, right):
    return lax.dot_general(left, right, (((1,), (1,)), ((), ())), preferred_element_type=full)


def segment_numbers(positions, lengths):
    row_ends = jnp.cumsum(lengths)
    return jnp.sum((positions[..., None] >= row_ends).astype(jnp.int32), axis=-1)


def probabilities(query, keys, mask):
    scores = matmul_right_t(query, keys) * SCALE
    scores = jnp.where(mask > 0, scores, -1e30)
    weights = jnp.exp(scores - jnp.max(scores, axis=-1, keepdims=True))
    return weights / jnp.sum(weights, axis=-1, keepdims=True)


def attend_kernel(place, q_ref, k_ref, v_ref, kp_ref, vp_ref, mask_ref, out_ref):
    mask = mask_ref[0]
    for head in range(q_ref.shape[1] // HEAD):
        at = slice(head * HEAD, (head + 1) * HEAD)
        keys = jnp.concatenate([kp_ref[:, at], k_ref[:, at]], axis=0)
        values = jnp.concatenate([vp_ref[:, at], v_ref[:, at]], axis=0)
        probs = probabilities(q_ref[:, at], keys, mask)
        out_ref[:, at] = matmul(probs.astype(low), values).astype(low)


def attend_back_kernel(
    place, q_ref, k_ref, v_ref, kp_ref, vp_ref, mask_ref, gm_ref, grads_ref, tail_ref, halo_ref, carry
):
    step = pl.program_id(0)
    mask = mask_ref[0]
    wide = q_ref.shape[1]

    @pl.when(step == 0)
    def _():
        carry[...] = jnp.zeros_like(carry)

    for head in range(wide // HEAD):
        at = slice(head * HEAD, (head + 1) * HEAD)
        query = q_ref[:, at]
        keys = jnp.concatenate([kp_ref[:, at], k_ref[:, at]], axis=0)
        values = jnp.concatenate([vp_ref[:, at], v_ref[:, at]], axis=0)
        grad_mixed = gm_ref[:, at]
        probs = probabilities(query, keys, mask)
        grad_probs = matmul_right_t(grad_mixed, values)
        inner = jnp.sum(probs * grad_probs, axis=-1, keepdims=True)
        grad_scores = (probs * (grad_probs - inner)).astype(low)
        grads_ref[:, at] = (matmul(grad_scores, keys) * SCALE).astype(low)
        grad_keys = matmul_left_t(grad_scores, query) * SCALE
        grad_values = matmul_left_t(probs.astype(low), grad_mixed)
        for which, grad in ((0, grad_keys), (1, grad_values)):
            col = which * wide + head * HEAD
            here = slice(col, col + HEAD)
            there = slice(wide + col, wide + col + HEAD)
            last = grad[BLOCK:] + carry[:, here]
            grads_ref[: BLOCK - WIN, there] = grad[WIN:BLOCK].astype(low)
            grads_ref[BLOCK - WIN :, there] = last.astype(low)

            @pl.when(step == 0)
            def _(last=last, here=here):
                tail_ref[:, here] = last

            carry[:, here] = grad[:WIN]

    @pl.when(step == N_TEAM - 1)
    def _():
        halo_ref[...] = carry[...].astype(low)


def attention_specs(wide):
    def block(rows, column, first):
        return pl.BlockSpec((rows, wide), lambda s, place: (place[first + s], column))

    return [
        block(BLOCK, 0, 0),
        block(BLOCK, 1, 0),
        block(BLOCK, 2, 0),
        block(WIN, 1, N_TEAM),
        block(WIN, 2, N_TEAM),
        pl.BlockSpec((1, BLOCK, BLOCK + WIN), lambda s, place: (place[s], 0, 0)),
    ]


def attend(place, qkv, mask):
    wide = qkv.shape[1] // 3
    return pl.pallas_call(
        attend_kernel,
        grid_spec=pltpu.PrefetchScalarGridSpec(
            num_scalar_prefetch=1,
            grid=(N_TEAM,),
            in_specs=attention_specs(wide),
            out_specs=pl.BlockSpec((BLOCK, wide), lambda s, place: (place[s], 0)),
        ),
        out_shape=jax.ShapeDtypeStruct((N_TEAM * BLOCK, wide), low),
        compiler_params=pltpu.CompilerParams(vmem_limit_bytes=16 << 20),
    )(place, qkv, qkv, qkv, qkv, qkv, mask)


def attend_back(place, qkv, mask, grad_mixed):
    wide = qkv.shape[1] // 3
    flip = lambda spec: pl.BlockSpec(
        spec.block_shape, lambda s, place: spec.index_map(N_TEAM - 1 - s, place)
    )
    by_block = lambda width: pl.BlockSpec((BLOCK, width), lambda s, place: (place[N_TEAM - 1 - s], 0))
    once = pl.BlockSpec((WIN, 2 * wide), lambda s, place: (0, 0))
    return pl.pallas_call(
        attend_back_kernel,
        grid_spec=pltpu.PrefetchScalarGridSpec(
            num_scalar_prefetch=1,
            grid=(N_TEAM,),
            in_specs=[flip(spec) for spec in attention_specs(wide)] + [by_block(wide)],
            out_specs=[by_block(3 * wide), once, once],
            scratch_shapes=[pltpu.VMEM((WIN, 2 * wide), full)],
        ),
        out_shape=[
            jax.ShapeDtypeStruct((N_TEAM * BLOCK, 3 * wide), low),
            jax.ShapeDtypeStruct((WIN, 2 * wide), full),
            jax.ShapeDtypeStruct((WIN, 2 * wide), low),
        ],
        compiler_params=pltpu.CompilerParams(vmem_limit_bytes=16 << 20),
    )(place, qkv, qkv, qkv, qkv, qkv, mask, grad_mixed)


def norm_backward(grad_normed, inputs, scale_rows, gain):
    weighted = grad_normed * gain
    gain_term = jnp.sum(grad_normed * inputs * scale_rows, axis=0)
    input_term = scale_rows * weighted - inputs * scale_rows**3 * jnp.mean(
        weighted * inputs, axis=-1, keepdims=True
    )
    return (gain_term, input_term)


def fleet_reduce(terms):
    return lax.psum_scatter(terms.astype(low), (*FLEET, "g"), scatter_dimension=0, tiled=True)


def body(
    tokens, lengths, norm_gain, w_query, w_key, w_value, w_out, mlp_gain, w_gate, w_up, w_down, cotangent
):
    rows, width = tokens.shape
    shard = w_query.shape[0]
    team_wide = width // N_TEAM
    unit_rows = w_down.shape[0]
    unit_pad = -(-unit_rows // 32) * 32
    units = N_FLEET * unit_pad
    z, c = lax.axis_index("z"), lax.axis_index("c")
    fleet = lax.axis_index(FLEET)

    gains = lax.all_gather(jnp.concatenate([norm_gain, mlp_gain])[None], SEQ, axis=0, tiled=True)
    gain_one = gains[:, :shard].reshape(width).astype(full)
    gain_two = gains[:, shard:].reshape(width).astype(full)
    out_there = swapped(w_out)
    qkv_cut = jnp.stack([w_query, w_key, w_value], axis=1).reshape(shard, 3, N_TEAM, team_wide)
    qkv_cut = qkv_cut.transpose(2, 0, 1, 3).reshape(N_TEAM, shard, 3 * team_wide)
    qkv_cut = lax.all_to_all(qkv_cut, TEAM, 0, 0, tiled=True).reshape(N_TEAM * shard, 3 * team_wide)
    out_cut = out_there.reshape(shard, N_TEAM, team_wide).transpose(1, 0, 2)
    out_cut = out_cut.reshape(N_TEAM * shard, team_wide)
    attn = lax.all_gather(jnp.concatenate([qkv_cut, out_cut], axis=1), FLEET, axis=0, tiled=True)
    w_qkv = attn[:, : 3 * team_wide]
    w_out_team = attn[:, 3 * team_wide :].reshape(N_FLEET, N_TEAM, shard, team_wide)
    w_out_team = w_out_team.transpose(0, 2, 1, 3).reshape(N_FLEET * shard, width)

    def units_cut(weight):
        cut = weight.reshape(shard, N_FLEET, N_TEAM, unit_rows)
        cut = jnp.pad(cut, ((0, 0), (0, 0), (0, 0), (0, unit_pad - unit_rows)))
        return cut.transpose(2, 0, 1, 3).reshape(N_TEAM, shard, units)

    gate_up_cut = jnp.concatenate([units_cut(w_gate), units_cut(w_up)], axis=2)
    gate_up_cut = lax.all_to_all(gate_up_cut, TEAM, 0, 0, tiled=True)
    w_gate_up = lax.all_gather(
        gate_up_cut.reshape(N_TEAM * shard, 2 * units), FLEET, axis=0, tiled=True
    )
    down_cut = jnp.pad(w_down, ((0, unit_pad - unit_rows), (0, 0)))
    w_down_team = lax.all_gather(down_cut, FLEET, axis=0, tiled=True)

    order = jnp.arange(N_TEAM, dtype=jnp.int32)
    spot = (jnp.bitwise_xor(order % N_C, c) * N_Z + (order // N_C - z) % N_Z).astype(jnp.int32)
    before = jnp.concatenate([jnp.full((1,), 2 * N_TEAM, jnp.int32), 2 * spot[:-1] + 1])
    place = jnp.concatenate([spot, before])
    last_at = spot[N_TEAM - 1] * BLOCK + BLOCK - WIN
    kept = jnp.arange(N_TEAM, dtype=jnp.int32)
    kept_block = N_C * ((kept % N_Z + z) % N_Z) + jnp.bitwise_xor(kept // N_Z, c)
    first_pos = (fleet * N_TEAM + kept_block) * BLOCK
    query_pos = first_pos[:, None] + jnp.arange(BLOCK, dtype=jnp.int32)
    key_pos = first_pos[:, None] - WIN + jnp.arange(BLOCK + WIN, dtype=jnp.int32)
    query_segs = segment_numbers(query_pos, lengths[0])
    key_segs = jnp.where(key_pos >= 0, segment_numbers(key_pos, lengths[0]), -1)
    distance = query_pos[:, :, None] - key_pos[:, None, :]
    mask = (distance >= 0) & (distance < WIN) & (query_segs[:, :, None] == key_segs[:, None, :])
    mask = mask.astype(full)

    token_rows = team_gather(tokens)
    halo = along_line(lax.dynamic_slice_in_dim(token_rows, last_at, WIN, 0), 1)
    token_rows = jnp.concatenate([token_rows, halo], axis=0).astype(full)
    normed = (token_rows * inverse_rms(token_rows) * gain_one).astype(low)
    qkv = matmul(normed, w_qkv).astype(low)
    mixed = attend(place, qkv, mask)
    inputs = tokens.astype(full)
    hidden = inputs + team_scatter(matmul(mixed, w_out_team))

    cotangents = team_gather(cotangent)
    scale_two = inverse_rms(hidden)
    again = team_gather((hidden * scale_two * gain_two).astype(low))
    both = matmul(again, w_gate_up)
    gate, up = both[:, :units], both[:, units:]
    sigmoid = jax.nn.sigmoid(gate)
    silu = gate * sigmoid
    activated = (silu * up).astype(low)
    grad_act = matmul_right_t(cotangents, w_down_team)
    grad_gate = (grad_act * up * sigmoid * (1.0 + gate * (1.0 - sigmoid))).astype(low)
    grad_up = (grad_act * silu).astype(low)
    grad_both = jnp.concatenate([grad_gate, grad_up], axis=1)
    grad_again = team_scatter(matmul_right_t(grad_both, w_gate_up))
    down_sum = fleet_reduce(matmul_left_t(activated, cotangents))
    pair_rows = shard // 2
    gate_up_term = matmul_left_t(again, grad_both).astype(low)
    gate_up_term = gate_up_term.reshape(N_FLEET, N_TEAM, 2, pair_rows, 2 * units)
    gate_up_term = gate_up_term.transpose(0, 2, 1, 3, 4).reshape(width, 2 * units)
    gate_up_sum = fleet_reduce(gate_up_term)

    gain_two_term, through_second = norm_backward(grad_again, hidden, scale_two, gain_two)
    grad_hidden = cotangent.astype(full) + through_second
    hidden_low = team_gather(grad_hidden.astype(low))
    outputs = (hidden + team_scatter(matmul(activated, w_down_team))).astype(low)

    grad_mixed = matmul_right_t(hidden_low, w_out_team).astype(low)
    grad_qkv, tail, halo_grads = attend_back(place, qkv, mask, grad_mixed)
    tail = tail + along_line(halo_grads, -1).astype(full)
    grad_qkv = lax.dynamic_update_slice(grad_qkv, tail.astype(low), (last_at, team_wide))
    out_term = matmul_left_t(mixed, hidden_low)
    grad_normed = team_scatter(matmul_right_t(grad_qkv, w_qkv))
    qkv_term = matmul_left_t(normed[: N_TEAM * BLOCK], grad_qkv).astype(low)
    qkv_term = qkv_term.reshape(N_FLEET, N_TEAM, 2, pair_rows, 3 * team_wide)
    qkv_term = qkv_term.transpose(0, 2, 1, 3, 4).reshape(width, 3 * team_wide)
    out_term = out_term.astype(low).reshape(N_FLEET, 2, pair_rows, N_TEAM, team_wide)
    out_term = out_term.transpose(0, 1, 3, 2, 4).reshape(width, team_wide)
    attn_sum = fleet_reduce(jnp.concatenate([qkv_term, out_term], axis=1))
    gain_one_term, through_first = norm_backward(grad_normed, inputs, inverse_rms(inputs), gain_one)
    input_grad = grad_hidden + through_first

    mine = lax.axis_index("g") == 0

    def both_halves(value):
        other = from_ahead(value, "g", 1)
        return jnp.concatenate(
            [jnp.where(mine, value, other), jnp.where(mine, other, value)], axis=-2
        )

    def to_owners(sums, blocks):
        sums = lax.all_to_all(sums.reshape(N_TEAM, pair_rows, sums.shape[1]), TEAM, 0, 0, tiled=True)
        sums = both_halves(sums)
        return jnp.split(sums, blocks, axis=2)

    def columns(block):
        return block.transpose(1, 0, 2).reshape(shard, width).astype(full)

    def unit_columns(block):
        block = block.reshape(N_TEAM, shard, N_FLEET, unit_pad)[..., :unit_rows]
        return block.transpose(1, 2, 0, 3).reshape(shard, N_FLEET * N_TEAM * unit_rows).astype(full)

    gate_cols, up_cols = to_owners(gate_up_sum, 2)
    down_grad = both_halves(down_sum)[:unit_rows].astype(full)
    query_cols, key_cols, value_cols = to_owners(attn_sum[:, : 3 * team_wide], 3)
    out_grad = swapped(attn_sum[:, 3 * team_wide :])
    out_grad = both_halves(out_grad.reshape(N_TEAM, pair_rows, team_wide))
    gain_terms = jnp.concatenate(
        [gain_one_term.reshape(-1, shard), gain_two_term.reshape(-1, shard)], axis=1
    )
    gain_sum = jnp.sum(lax.all_to_all(gain_terms, SEQ, 0, 0, tiled=True), axis=0)
    gain_sum = gain_sum + from_ahead(gain_sum, "g", 1)
    return (
        outputs,
        input_grad,
        gain_sum[:shard],
        columns(query_cols),
        columns(key_cols),
        columns(value_cols),
        columns(out_grad),
        gain_sum[shard:],
        unit_columns(gate_cols),
        unit_columns(up_cols),
        down_grad,
    )


def solution(mesh):
    fine = Mesh(mesh.devices.reshape(2, 2, 4, 4, 2), ALL)
    return jax.shard_map(
        body,
        mesh=fine,
        in_specs=(
            P(ALL, None),
            P("g", None),
            P(SEQ),
            P(SEQ, None),
            P(SEQ, None),
            P(SEQ, None),
            P(SEQ, None),
            P(SEQ),
            P(SEQ, None),
            P(SEQ, None),
            P(SEQ, None),
            P(ALL, None),
        ),
        out_specs=(
            P(ALL, None),
            P(ALL, None),
            P(SEQ),
            P(SEQ, None),
            P(SEQ, None),
            P(SEQ, None),
            P(SEQ, None),
            P(SEQ),
            P(SEQ, None),
            P(SEQ, None),
            P(SEQ, None),
        ),
        check_vma=False,
    )
```

```python
import functools

import jax
import jax.numpy as jnp
from jax import lax
from jax.experimental import pallas as pl
from jax.experimental.pallas import tpu as pltpu
from jax.sharding import Mesh
from jax.sharding import PartitionSpec as P

HEAD = 128
WIN = 64
BLOCK = 128
epsilon = 1e-06

TEAM = ("z", "c")
FLEET = ("yl", "x")
SEQ = ("yl", "x", "z", "c")
ALL = ("g", "yl", "x", "z", "c")
N_X, N_Z, N_C, N_TEAM, N_FLEET = 4, 4, 2, 8, 8
SCALE = HEAD ** (-0.5)
low = jnp.bfloat16
full = jnp.float32


def from_ahead(value, axis, by):
    n = lax.axis_size(axis)
    return lax.ppermute(value, axis, [((i + by) % n, i) for i in range(n)])


def along_line(value, by):
    return lax.ppermute(
        value, FLEET, [(i, i + by) for i in range(N_FLEET) if 0 <= i + by < N_FLEET]
    )


def swapped(value, across=0):
    n = N_FLEET * N_TEAM
    pairs = [(N_TEAM * f + t, N_TEAM * t + f) for f in range(N_FLEET) for t in range(N_TEAM)]
    return lax.ppermute(value, ALL, [(g * n + a, (g ^ across) * n + b) for g in range(2) for a, b in pairs])


def z_gather(value):
    return [value] + [from_ahead(value, "z", k) for k in (1, 2, 3)]


def z_sum(blocks):
    return blocks[0] + sum(from_ahead(blocks[k].astype(low), "z", -k).astype(full) for k in (1, 2, 3))


def core_sum(left, right):
    there = from_ahead(right(left[1]).astype(low), "c", 1)
    pair = right(left[0]) + there.astype(full)
    rows = pair.shape[0] // N_Z
    return [pair[k * rows : (k + 1) * rows] for k in range(N_Z)]


def in_order(pieces):
    rows = pieces[0][0].shape[0]
    x, yl = lax.axis_index("x"), lax.axis_index("yl")
    whole = jnp.zeros((N_FLEET * rows, pieces[0][0].shape[1]), low)
    for side in range(2):
        for k in (0, 1, 3, 2):
            place = ((yl ^ side) * N_X + (x + k) % N_X) * rows
            whole = lax.dynamic_update_slice(whole, pieces[side][k], (place, 0))
    return whole


def inverse_rms(values):
    return lax.rsqrt(jnp.mean(values * values, axis=-1, keepdims=True) + epsilon)


def matmul(left, right):
    return jnp.dot(left, right, preferred_element_type=full)


def matmul_left_t(left, right):
    return lax.dot_general(left, right, (((0,), (0,)), ((), ())), preferred_element_type=full)


def matmul_right_t(left, right):
    return lax.dot_general(left, right, (((1,), (1,)), ((), ())), preferred_element_type=full)


def cut_kernel(unit_rows, q_ref, k_ref, v_ref, gate_ref, up_ref, gain_ref, out_ref):
    wide = q_ref.shape[1] // N_TEAM
    lanes = gain_ref.shape[1]
    units = (out_ref.shape[2] - 3 * wide - lanes) // 2
    pad = units // N_FLEET
    at_gate = 3 * wide + lanes
    out_ref[:, :, at_gate:] = jnp.zeros((N_TEAM, q_ref.shape[0], 2 * units), low)
    for t in range(N_TEAM):
        for i, ref in enumerate((q_ref, k_ref, v_ref)):
            out_ref[t, :, i * wide : (i + 1) * wide] = ref[:, t * wide : (t + 1) * wide]
        out_ref[t, :, 3 * wide : at_gate] = gain_ref[...]
        for i, ref in enumerate((gate_ref, up_ref)):
            for f in range(N_FLEET):
                at = at_gate + i * units + f * pad
                first = (f * N_TEAM + t) * unit_rows
                out_ref[t, :, at : at + unit_rows] = ref[:, first : first + unit_rows]


def cut_for_team(w_query, w_key, w_value, w_gate, w_up, gains, unit_rows, units):
    shard, width = w_query.shape
    columns = 3 * width // N_TEAM + gains.shape[1] + 2 * units
    return pl.pallas_call(
        functools.partial(cut_kernel, unit_rows),
        out_shape=jax.ShapeDtypeStruct((N_TEAM, shard, columns), low),
        compiler_params=pltpu.CompilerParams(vmem_limit_bytes=16 << 20),
    )(w_query, w_key, w_value, w_gate, w_up, gains)


def norm_kernel(mine_ref, other_ref, halo_ref, gain_ref, out_ref):
    gain = gain_ref[...].astype(full).T[:1]
    at = 0
    for ref in (mine_ref, other_ref, halo_ref):
        for first in range(0, ref.shape[0], 16):
            values = ref[first : first + 16].astype(full)
            out_ref[at + first : at + first + 16] = (values * inverse_rms(values) * gain).astype(low)
        at += ref.shape[0]


def normalised(mine, other, halo, gain_columns):
    rows = mine.shape[0] + other.shape[0] + halo.shape[0]
    return pl.pallas_call(
        norm_kernel,
        out_shape=jax.ShapeDtypeStruct((rows, mine.shape[1]), low),
        compiler_params=pltpu.CompilerParams(vmem_limit_bytes=32 << 20),
    )(mine, other, halo, gain_columns)


TILE = 256


def terms_kernel(x0_ref, x1_ref, dy0_ref, dy1_ref, act0_ref, act1_ref, grad0_ref, grad1_ref, out_ref, down):
    step = pl.program_id(0)
    units = act0_ref.shape[1]
    pad = units // N_FLEET
    block = x0_ref.shape[1]

    @pl.when(step == 0)
    def _():
        for first in range(0, units, TILE):
            at = slice(first, first + TILE)
            down[at] = (
                matmul_left_t(act0_ref[:, at], dy0_ref[...]) + matmul_left_t(act1_ref[:, at], dy1_ref[...])
            ).astype(low)

    for i in range(2):
        at = slice(i * units, (i + 1) * units)
        term = matmul_left_t(x0_ref[...], grad0_ref[:, at]) + matmul_left_t(x1_ref[...], grad1_ref[:, at])
        term = term.astype(low)
        for row in range(0, block, 32):
            for g in range(2):
                out_ref[g, 0, row // 2 : row // 2 + 16, at] = term[row + 16 * g : row + 16 * g + 16]
    rows = down[pl.ds(pl.multiple_of(step * pad, 16), pad)]
    for g in range(2):
        for (row, col), (to, lane) in down_chunks(pad // 2, rows.shape[1], 2 * units):
            first = g * (pad // 2) + row
            out_ref[g, 0, block // 2 + to : block // 2 + to + 16, lane : lane + 512] = rows[
                first : first + 16, col : col + 512
            ]


def down_chunks(rows, width, wide):
    packed = rows * width // wide
    places = [(row, col) for col in range(0, width, 512) for row in range(0, rows, 16)]
    return [(place, (16 * i % packed, 16 * i // packed * 512)) for i, place in enumerate(places)]


def unpack_down(packed, rows, width):
    parts = {
        place: packed[to : to + 16, lane : lane + 512]
        for place, (to, lane) in down_chunks(rows, width, packed.shape[1])
    }
    return jnp.concatenate(
        [jnp.concatenate([parts[row, col] for col in range(0, width, 512)], axis=1) for row in range(0, rows, 16)],
        axis=0,
    )


def feed_terms(rows, dy_rows, activated, grad_both):
    half, width = rows[0].shape
    units = activated[0].shape[1]
    block = width // N_FLEET
    tall = block // 2 + units // N_FLEET // 2 * width // (2 * units)
    whole = lambda wide: pl.BlockSpec((half, wide), lambda s: (0, 0))
    cut = pl.BlockSpec((half, block), lambda s: (0, s))
    return pl.pallas_call(
        terms_kernel,
        grid=(N_FLEET,),
        in_specs=[cut] * 2 + [whole(width)] * 2 + [whole(units)] * 2 + [whole(2 * units)] * 2,
        out_specs=pl.BlockSpec((2, 1, tall, 2 * units), lambda s: (0, s, 0, 0)),
        out_shape=jax.ShapeDtypeStruct((2, N_FLEET, tall, 2 * units), low),
        scratch_shapes=[pltpu.VMEM((units, width), low)],
        compiler_params=pltpu.CompilerParams(vmem_limit_bytes=56 << 20),
        cost_estimate=pl.CostEstimate(flops=1, bytes_accessed=1, transcendentals=0),
    )(*rows, *dy_rows, *activated, *grad_both)


def segment_numbers(positions, lengths):
    row_ends = jnp.cumsum(lengths)
    return jnp.sum((positions[..., None] >= row_ends).astype(jnp.int32), axis=-1)


def probabilities(query, keys, mask):
    scores = matmul_right_t(query, keys) * SCALE
    scores = jnp.where(mask > 0, scores, -1e30)
    weights = jnp.exp(scores - jnp.max(scores, axis=-1, keepdims=True))
    return weights / jnp.sum(weights, axis=-1, keepdims=True)


def attend_kernel(place, q_ref, k_ref, v_ref, kp_ref, vp_ref, mask_ref, out_ref):
    mask = mask_ref[0]
    for head in range(q_ref.shape[1] // HEAD):
        at = slice(head * HEAD, (head + 1) * HEAD)
        keys = jnp.concatenate([kp_ref[:, at], k_ref[:, at]], axis=0)
        values = jnp.concatenate([vp_ref[:, at], v_ref[:, at]], axis=0)
        probs = probabilities(q_ref[:, at], keys, mask)
        out_ref[:, at] = matmul(probs.astype(low), values).astype(low)


def attend_back_kernel(
    place, q_ref, k_ref, v_ref, kp_ref, vp_ref, mask_ref, gm_ref, grads_ref, tail_ref, halo_ref, carry
):
    step = pl.program_id(0)
    mask = mask_ref[0]
    wide = q_ref.shape[1]

    @pl.when(step == 0)
    def _():
        carry[...] = jnp.zeros_like(carry)

    for head in range(wide // HEAD):
        at = slice(head * HEAD, (head + 1) * HEAD)
        query = q_ref[:, at]
        keys = jnp.concatenate([kp_ref[:, at], k_ref[:, at]], axis=0)
        values = jnp.concatenate([vp_ref[:, at], v_ref[:, at]], axis=0)
        grad_mixed = gm_ref[:, at]
        probs = probabilities(query, keys, mask)
        grad_probs = matmul_right_t(grad_mixed, values)
        inner = jnp.sum(probs * grad_probs, axis=-1, keepdims=True)
        grad_scores = (probs * (grad_probs - inner)).astype(low)
        grads_ref[:, at] = (matmul(grad_scores, keys) * SCALE).astype(low)
        grad_keys = matmul_left_t(grad_scores, query) * SCALE
        grad_values = matmul_left_t(probs.astype(low), grad_mixed)
        for which, grad in ((0, grad_keys), (1, grad_values)):
            col = which * wide + head * HEAD
            here = slice(col, col + HEAD)
            there = slice(wide + col, wide + col + HEAD)
            last = grad[BLOCK:] + carry[:, here]
            grads_ref[: BLOCK - WIN, there] = grad[WIN:BLOCK].astype(low)
            grads_ref[BLOCK - WIN :, there] = last.astype(low)

            @pl.when(step == 0)
            def _(last=last, here=here):
                tail_ref[:, here] = last

            carry[:, here] = grad[:WIN]

    @pl.when(step == N_TEAM - 1)
    def _():
        halo_ref[...] = carry[...].astype(low)


def attention_specs(wide):
    def block(rows, column, first):
        return pl.BlockSpec((rows, wide), lambda s, place: (place[first + s], column))

    return [
        block(BLOCK, 0, 0),
        block(BLOCK, 1, 0),
        block(BLOCK, 2, 0),
        block(WIN, 1, N_TEAM),
        block(WIN, 2, N_TEAM),
        pl.BlockSpec((1, BLOCK, BLOCK + WIN), lambda s, place: (place[s], 0, 0)),
    ]


def attend(place, qkv, mask):
    wide = qkv.shape[1] // 3
    return pl.pallas_call(
        attend_kernel,
        grid_spec=pltpu.PrefetchScalarGridSpec(
            num_scalar_prefetch=1,
            grid=(N_TEAM,),
            in_specs=attention_specs(wide),
            out_specs=pl.BlockSpec((BLOCK, wide), lambda s, place: (place[s], 0)),
        ),
        out_shape=jax.ShapeDtypeStruct((N_TEAM * BLOCK, wide), low),
        compiler_params=pltpu.CompilerParams(vmem_limit_bytes=16 << 20),
    )(place, qkv, qkv, qkv, qkv, qkv, mask)


def attend_back(place, qkv, mask, grad_mixed):
    wide = qkv.shape[1] // 3
    flip = lambda spec: pl.BlockSpec(
        spec.block_shape, lambda s, place: spec.index_map(N_TEAM - 1 - s, place)
    )
    by_block = lambda width: pl.BlockSpec((BLOCK, width), lambda s, place: (place[N_TEAM - 1 - s], 0))
    once = pl.BlockSpec((WIN, 2 * wide), lambda s, place: (0, 0))
    return pl.pallas_call(
        attend_back_kernel,
        grid_spec=pltpu.PrefetchScalarGridSpec(
            num_scalar_prefetch=1,
            grid=(N_TEAM,),
            in_specs=[flip(spec) for spec in attention_specs(wide)] + [by_block(wide)],
            out_specs=[by_block(3 * wide), once, once],
            scratch_shapes=[pltpu.VMEM((WIN, 2 * wide), full)],
        ),
        out_shape=[
            jax.ShapeDtypeStruct((N_TEAM * BLOCK, 3 * wide), low),
            jax.ShapeDtypeStruct((WIN, 2 * wide), full),
            jax.ShapeDtypeStruct((WIN, 2 * wide), low),
        ],
        compiler_params=pltpu.CompilerParams(vmem_limit_bytes=16 << 20),
    )(place, qkv, qkv, qkv, qkv, qkv, mask, grad_mixed)


def norm_backward(grad_normed, inputs, scale_rows, gain):
    weighted = grad_normed * gain
    gain_term = jnp.sum(grad_normed * inputs * scale_rows, axis=0)
    input_term = scale_rows * weighted - inputs * scale_rows**3 * jnp.mean(
        weighted * inputs, axis=-1, keepdims=True
    )
    return (gain_term, input_term)


def body(
    tokens, lengths, norm_gain, w_query, w_key, w_value, w_out, mlp_gain, w_gate, w_up, w_down, cotangent
):
    rows, width = tokens.shape
    shard = w_query.shape[0]
    team_wide = width // N_TEAM
    unit_rows = w_down.shape[0]
    unit_pad = -(-unit_rows // 32) * 32
    units = N_FLEET * unit_pad
    x, yl, z, c = [lax.axis_index(axis) for axis in ("x", "yl", "z", "c")]
    fleet = lax.axis_index(FLEET)

    inputs = tokens.astype(full)
    down_cut = jnp.pad(w_down, ((0, unit_pad - unit_rows), (0, 0)))
    w_down_team = lax.all_gather(down_cut, FLEET, axis=0, tiled=True)
    gains = jnp.concatenate([norm_gain[:, None], mlp_gain[:, None], jnp.zeros((shard, 126), low)], axis=1)
    cut = cut_for_team(w_query, w_key, w_value, w_gate, w_up, gains, unit_rows, units)
    cut = lax.all_to_all(cut, TEAM, 0, 0, tiled=True).reshape(N_TEAM * shard, -1)
    out_there = swapped(w_out)
    cut, out_there, tokens_later, cotangent_later = lax.optimization_barrier((cut, out_there, tokens, cotangent))
    at_gate = 3 * team_wide + gains.shape[1]
    out_cut = out_there.reshape(shard, N_TEAM, team_wide).transpose(1, 0, 2)
    out_cut = out_cut.reshape(N_TEAM * shard, team_wide)
    attn = jnp.concatenate([cut[:, :at_gate], out_cut], axis=1)
    along_y = lambda value, by: from_ahead(value, ("g", "yl"), by)
    attn_x = [attn, from_ahead(attn, "x", 1), None, from_ahead(attn, "x", 3)]
    attn_y = [along_y(attn, 1)]
    x_mine = [tokens_later, from_ahead(tokens_later, "z", 1), None, from_ahead(tokens_later, "z", 3)]
    attn_x, attn_y, x_mine = lax.optimization_barrier((attn_x, attn_y, x_mine))
    attn_y += [along_y(attn_x[1], -1), None, along_y(attn_x[3], 1)]
    attn_x[2] = from_ahead(attn_x[0], "x", 2)
    x_mine[2] = from_ahead(x_mine[0], "z", 2)
    attn_x, attn_y, x_mine, cotangent_later = lax.optimization_barrier((attn_x, attn_y, x_mine, cotangent_later))
    low_half = shard * N_TEAM // 2
    attn_y[2] = jnp.concatenate(
        [along_y(attn_x[2][:low_half], 1), along_y(attn_x[2][low_half:], -1)], axis=0
    )
    x_mine = jnp.concatenate(x_mine, axis=0)
    x_other = from_ahead(x_mine, "c", 1)
    dy_mine = [cotangent_later, from_ahead(cotangent_later, "z", 1), None, from_ahead(cotangent_later, "z", 3)]
    attn_x, attn_y, x_other, dy_mine, gate_up = lax.optimization_barrier(
        (attn_x, attn_y, x_other, dy_mine, cut[:, at_gate:])
    )
    w_gate_up = lax.all_gather(gate_up, FLEET, axis=0, tiled=True)
    dy_mine[2] = from_ahead(dy_mine[0], "z", 2)
    attn = in_order([attn_x, attn_y])
    w_qkv = attn[:, : 3 * team_wide]
    gain_columns = attn[:, 3 * team_wide : at_gate]
    gain_one = gain_columns[:, 0].reshape(1, width).astype(full)
    gain_two = gain_columns[:, 1].reshape(1, width).astype(full)
    w_out_team = attn[:, at_gate:].reshape(N_FLEET, N_TEAM, shard, team_wide)
    w_out_team = w_out_team.transpose(0, 2, 1, 3).reshape(N_FLEET * shard, width)

    order = jnp.arange(N_TEAM, dtype=jnp.int32)
    spot = (jnp.bitwise_xor(order % N_C, c) * N_Z + (order // N_C - z) % N_Z).astype(jnp.int32)
    before = jnp.concatenate([jnp.full((1,), 2 * N_TEAM, jnp.int32), 2 * spot[:-1] + 1])
    place = jnp.concatenate([spot, before])
    last_at = spot[N_TEAM - 1] * BLOCK + BLOCK - WIN
    kept = jnp.arange(N_TEAM, dtype=jnp.int32)
    kept_block = N_C * ((kept % N_Z + z) % N_Z) + jnp.bitwise_xor(kept // N_Z, c)
    first_pos = (fleet * N_TEAM + kept_block) * BLOCK
    query_pos = first_pos[:, None] + jnp.arange(BLOCK, dtype=jnp.int32)
    key_pos = first_pos[:, None] - WIN + jnp.arange(BLOCK + WIN, dtype=jnp.int32)
    query_segs = segment_numbers(query_pos, lengths[0])
    key_segs = jnp.where(key_pos >= 0, segment_numbers(key_pos, lengths[0]), -1)
    distance = query_pos[:, :, None] - key_pos[:, None, :]
    mask = (distance >= 0) & (distance < WIN) & (query_segs[:, :, None] == key_segs[:, None, :])
    mask = mask.astype(full)

    half = N_Z * BLOCK
    last_of = lambda rows: lax.dynamic_slice_in_dim(rows, last_at % half, WIN, 0)
    halo = along_line(jnp.where(last_at < half, last_of(x_mine), last_of(x_other)), 1)
    normed = normalised(x_mine, x_other, halo, gain_columns)
    qkv = matmul(normed, w_qkv).astype(low)
    qkv, dy_mine = lax.optimization_barrier((qkv, dy_mine))
    dy_mine = jnp.concatenate(dy_mine, axis=0)
    dy_other = from_ahead(dy_mine, "c", 1)
    mixed = attend(place, qkv, mask)
    mixed, dy_other = lax.optimization_barrier((mixed, dy_other))
    halves = lambda rows: (rows[:half], rows[half : 2 * half])
    hidden = inputs + z_sum(core_sum(halves(mixed), lambda rows: matmul(rows, w_out_team)))

    scale_two = inverse_rms(hidden)
    again = [jnp.concatenate(z_gather((hidden * scale_two * gain_two).astype(low)), axis=0)]
    again.append(from_ahead(again[0], "c", 1))
    dy_rows, activated, grad_both = [dy_mine, dy_other], [], []
    for rows, dy in zip(again, dy_rows):
        both = matmul(rows, w_gate_up)
        gate, up = both[:, :units], both[:, units:]
        sigmoid = jax.nn.sigmoid(gate)
        silu = gate * sigmoid
        activated.append((silu * up).astype(low))
        grad_act = matmul_right_t(dy, w_down_team)
        grad_gate = (grad_act * up * sigmoid * (1.0 + gate * (1.0 - sigmoid))).astype(low)
        grad_up = (grad_act * silu).astype(low)
        grad_both.append(jnp.concatenate([grad_gate, grad_up], axis=1))
    again_blocks = core_sum(grad_both, lambda rows: matmul_right_t(rows, w_gate_up))
    again_blocks, activated, grad_both = lax.optimization_barrier((again_blocks, activated, grad_both))
    grad_again = z_sum(again_blocks)
    mlp_term = feed_terms(again, dy_rows, activated, grad_both)
    grad_again, mlp_term = lax.optimization_barrier((grad_again, mlp_term))
    mlp_sum = lax.psum_scatter(
        mlp_term.reshape(-1, 2 * units), ("g", *FLEET), scatter_dimension=0, tiled=True
    )

    gain_two_term, through_second = norm_backward(grad_again, hidden, scale_two, gain_two)
    grad_hidden = cotangent.astype(full) + through_second
    hidden_low = [jnp.concatenate(z_gather(grad_hidden.astype(low)), axis=0)]
    hidden_low.append(from_ahead(hidden_low[0], "c", 1))
    activated, hidden_low = lax.optimization_barrier((activated, hidden_low))
    output_blocks = core_sum(activated, lambda rows: matmul(rows, w_down_team))

    hidden_low = jnp.concatenate(hidden_low, axis=0)
    grad_mixed = matmul_right_t(hidden_low, w_out_team).astype(low)
    grad_qkv, tail, halo_grads = attend_back(place, qkv, mask, grad_mixed)
    tail = tail + along_line(halo_grads, -1).astype(full)
    grad_qkv = lax.dynamic_update_slice(grad_qkv, tail.astype(low), (last_at, team_wide))
    grad_qkv, output_blocks = lax.optimization_barrier((grad_qkv, output_blocks))
    outputs = (hidden + z_sum(output_blocks)).astype(low)
    qkv_term = matmul_left_t(normed[: 2 * half], grad_qkv).astype(low)
    out_term = matmul_left_t(mixed, hidden_low).astype(low).reshape(N_FLEET, shard, N_TEAM, team_wide)
    out_term = out_term.transpose(0, 2, 1, 3).reshape(width, team_wide)
    attn_term = jnp.concatenate([qkv_term, out_term], axis=1)
    attn_term, grad_qkv = lax.optimization_barrier((attn_term, grad_qkv))
    attn_sum = lax.psum_scatter(attn_term, FLEET, scatter_dimension=0, tiled=True)
    normed_blocks = core_sum(halves(grad_qkv), lambda rows: matmul_right_t(rows, w_qkv))
    normed_blocks, outputs = lax.optimization_barrier((normed_blocks, outputs))
    grad_normed = z_sum(normed_blocks)

    twice = lambda value: jnp.concatenate([value, value], axis=0)
    gate_up_sum = mlp_sum[: N_TEAM * shard // 2].reshape(N_TEAM, shard // 2, 2 * units)
    gate_up_sum = lax.all_to_all(twice(gate_up_sum), ("g", *TEAM), 0, 0, tiled=True)
    gate_up_sum = jnp.concatenate([gate_up_sum[:N_TEAM], gate_up_sum[N_TEAM:]], axis=1)
    down_sum = unpack_down(mlp_sum[N_TEAM * shard // 2 :], unit_pad // 2, width)
    down_there = from_ahead(down_sum, "g", 1)
    mine = lax.axis_index("g") == 0
    down_grad = jnp.concatenate(
        [jnp.where(mine, down_sum, down_there), jnp.where(mine, down_there, down_sum)], axis=0
    )
    down_grad = down_grad[:unit_rows].astype(full)
    grad_normed, gate_up_sum, down_grad = lax.optimization_barrier((grad_normed, gate_up_sum, down_grad))
    gain_one_term, through_first = norm_backward(grad_normed, inputs, inverse_rms(inputs), gain_one)
    input_grad = grad_hidden + through_first
    gain_terms = jnp.concatenate(
        [gain_one_term.reshape(-1, shard), gain_two_term.reshape(-1, shard)], axis=1
    )
    gain_sum = jnp.sum(lax.all_to_all(gain_terms, SEQ, 0, 0, tiled=True), axis=0)
    gain_sum = gain_sum + from_ahead(gain_sum, "g", 1)
    gain_sum, attn_sum, input_grad = lax.optimization_barrier((gain_sum, attn_sum, input_grad))

    def columns(block):
        return block.transpose(1, 0, 2).reshape(shard, width).astype(full)

    def unit_columns(block):
        block = block.reshape(N_TEAM, shard, N_FLEET, unit_pad)[..., :unit_rows]
        return block.transpose(1, 2, 0, 3).reshape(shard, N_FLEET * N_TEAM * unit_rows).astype(full)

    gate_cols, up_cols = jnp.split(gate_up_sum, 2, axis=2)
    qkv_sum = attn_sum[:, : 3 * team_wide].reshape(N_TEAM, shard, 3 * team_wide)
    qkv_sum = lax.all_to_all(twice(qkv_sum), ("g", *TEAM), 0, 0, tiled=True)
    qkv_sum = qkv_sum[:N_TEAM].astype(full) + qkv_sum[N_TEAM:].astype(full)
    query_cols, key_cols, value_cols = jnp.split(qkv_sum, 3, axis=2)
    out_sum = attn_sum[:, 3 * team_wide :].reshape(N_TEAM, shard, team_wide)
    out_grad = swapped(out_sum).astype(full) + swapped(out_sum, 1).astype(full)
    return (
        outputs,
        input_grad,
        gain_sum[:shard],
        columns(query_cols),
        columns(key_cols),
        columns(value_cols),
        columns(out_grad),
        gain_sum[shard:],
        unit_columns(gate_cols),
        unit_columns(up_cols),
        down_grad,
    )


def solution(mesh):
    fine = Mesh(mesh.devices.reshape(2, 2, 4, 4, 2), ALL)
    return jax.shard_map(
        body,
        mesh=fine,
        in_specs=(
            P(ALL, None),
            P("g", None),
            P(SEQ),
            P(SEQ, None),
            P(SEQ, None),
            P(SEQ, None),
            P(SEQ, None),
            P(SEQ),
            P(SEQ, None),
            P(SEQ, None),
            P(SEQ, None),
            P(ALL, None),
        ),
        out_specs=(
            P(ALL, None),
            P(ALL, None),
            P(SEQ),
            P(SEQ, None),
            P(SEQ, None),
            P(SEQ, None),
            P(SEQ, None),
            P(SEQ),
            P(SEQ, None),
            P(SEQ, None),
            P(SEQ, None),
        ),
        check_vma=False,
    )
```

```python
import functools

import jax
import jax.numpy as jnp
from jax import lax
from jax.experimental import pallas as pl
from jax.experimental.pallas import tpu as pltpu
from jax.sharding import Mesh
from jax.sharding import PartitionSpec as P

FILLS = pl.CostEstimate(flops=1, bytes_accessed=1, transcendentals=0)
HEAD = 128
WIN = 64
BLOCK = 128
epsilon = 1e-06

TEAM = ("z", "c")
FLEET = ("yl", "x")
SEQ = ("yl", "x", "z", "c")
ALL = ("g", "yl", "x", "z", "c")
N_X, N_Z, N_C, N_TEAM, N_FLEET = 4, 4, 2, 8, 8
SCALE = HEAD ** (-0.5)
low = jnp.bfloat16
full = jnp.float32


def from_ahead(value, axis, by):
    n = lax.axis_size(axis)
    return lax.ppermute(value, axis, [((i + by) % n, i) for i in range(n)])


def along_line(value, by):
    return lax.ppermute(
        value, FLEET, [(i, i + by) for i in range(N_FLEET) if 0 <= i + by < N_FLEET]
    )


def swapped(value, across=0):
    n = N_FLEET * N_TEAM
    pairs = [(N_TEAM * f + t, N_TEAM * t + f) for f in range(N_FLEET) for t in range(N_TEAM)]
    return lax.ppermute(value, ALL, [(g * n + a, (g ^ across) * n + b) for g in range(2) for a, b in pairs])


def z_gather(value):
    return [value] + [from_ahead(value, "z", k) for k in (1, 2, 3)]


def z_send(blocks):
    return [blocks[0]] + [from_ahead(blocks[k], "z", -k) for k in (1, 2, 3)]


def core_sum(left, right):
    there = right(left[1]).astype(low)
    return core_blocks(right(left[0]), there)


def inverse_rms(values):
    return lax.rsqrt(jnp.mean(values * values, axis=-1, keepdims=True) + epsilon)


def matmul(left, right):
    return jnp.dot(left, right, preferred_element_type=full)


def matmul_left_t(left, right):
    return lax.dot_general(left, right, (((0,), (0,)), ((), ())), preferred_element_type=full)


def matmul_right_t(left, right):
    return lax.dot_general(left, right, (((1,), (1,)), ((), ())), preferred_element_type=full)


def attn_cut_kernel(q_ref, k_ref, v_ref, gain_ref, out_ref):
    wide = q_ref.shape[1] // N_TEAM
    for t in range(N_TEAM):
        for i, ref in enumerate((q_ref, k_ref, v_ref)):
            out_ref[t, :, i * wide : (i + 1) * wide] = ref[:, t * wide : (t + 1) * wide]
        out_ref[t, :, 3 * wide :] = gain_ref[...]


def feed_cut_kernel(unit_rows, gate_ref, up_ref, out_ref):
    units = out_ref.shape[2] // 2
    pad = units // N_FLEET
    out_ref[...] = jnp.zeros(out_ref.shape, low)
    for t in range(N_TEAM):
        for i, ref in enumerate((gate_ref, up_ref)):
            for f in range(N_FLEET):
                at = i * units + f * pad
                first = (f * N_TEAM + t) * unit_rows
                out_ref[t, :, at : at + unit_rows] = ref[:, first : first + unit_rows]


def attn_cut(w_query, w_key, w_value, gains):
    shard, width = w_query.shape
    return pl.pallas_call(
        attn_cut_kernel,
        out_shape=jax.ShapeDtypeStruct((N_TEAM, shard, 3 * width // N_TEAM + gains.shape[1]), low),
        compiler_params=pltpu.CompilerParams(vmem_limit_bytes=8 << 20),
    )(w_query, w_key, w_value, gains)


def feed_cut(w_gate, w_up, unit_rows, units):
    return pl.pallas_call(
        functools.partial(feed_cut_kernel, unit_rows),
        out_shape=jax.ShapeDtypeStruct((N_TEAM, w_gate.shape[0], 2 * units), low),
        compiler_params=pltpu.CompilerParams(vmem_limit_bytes=8 << 20),
        cost_estimate=FILLS,
    )(w_gate, w_up)


def join_kernel(*refs):
    rows = refs[0].shape[0]
    for i, ref in enumerate(refs[:-1]):
        refs[-1][i * rows : (i + 1) * rows] = ref[...]


def join(blocks):
    rows, width = blocks[0].shape
    return pl.pallas_call(
        join_kernel,
        out_shape=jax.ShapeDtypeStruct((len(blocks) * rows, width), low),
        compiler_params=pltpu.CompilerParams(vmem_limit_bytes=8 << 20),
        cost_estimate=FILLS,
    )(*blocks)


def pair_kernel(here_ref, there_ref, own_ref, *block_refs):
    rows = own_ref.shape[0]
    for i, ref in enumerate((own_ref, *block_refs)):
        at = slice(i * rows, (i + 1) * rows)
        ref[...] = (here_ref[at] + there_ref[at].astype(full)).astype(ref.dtype)


def core_blocks(here, there):
    rows, width = here.shape[0] // N_Z, here.shape[1]
    return pl.pallas_call(
        pair_kernel,
        out_shape=[jax.ShapeDtypeStruct((rows, width), full)] + [jax.ShapeDtypeStruct((rows, width), low)] * 3,
        compiler_params=pltpu.CompilerParams(vmem_limit_bytes=12 << 20),
        cost_estimate=FILLS,
    )(here, from_ahead(there, "c", 1))


def norm_kernel(*refs):
    *block_refs, gain_ref, out_ref, rows_ref = refs
    rows_ref[...] = gain_ref[...].astype(full).T[: rows_ref.shape[0]]
    gain = rows_ref[:1]
    at = 0
    for ref in block_refs:
        for first in range(0, ref.shape[0], 16):
            values = ref[first : first + 16].astype(full)
            out_ref[at + first : at + first + 16] = (values * inverse_rms(values) * gain).astype(low)
        at += ref.shape[0]


def normalised(blocks, gain_columns):
    rows = sum(block.shape[0] for block in blocks)
    width = blocks[0].shape[1]
    return pl.pallas_call(
        norm_kernel,
        out_shape=[jax.ShapeDtypeStruct((rows, width), low), jax.ShapeDtypeStruct((8, width), full)],
        compiler_params=pltpu.CompilerParams(vmem_limit_bytes=14 << 20),
        cost_estimate=FILLS,
    )(*blocks, gain_columns)


TILE = 256


def feed_kernel(*refs):
    sources = refs[: 2 * N_Z]
    gate_ref, up_ref, down_ref, act_ref, grad_gate_ref, grad_up_ref, x_ref, dy_ref, arrived = refs[2 * N_Z :]
    rows = sources[0].shape[0]

    @pl.when(pl.program_id(0) == 0)
    def _():
        places = [ref.at[pl.ds(i * rows, rows)] for ref in (x_ref, dy_ref) for i in range(N_Z)]
        copies = [pltpu.make_async_copy(sources[i], places[i], arrived.at[i]) for i in range(2 * N_Z)]
        for copy in copies:
            copy.start()
        for copy in copies:
            copy.wait()

    gate = matmul(x_ref[...], gate_ref[...])
    up = matmul(x_ref[...], up_ref[...])
    grad_act = matmul_right_t(dy_ref[...], down_ref[...])
    sigmoid = jax.nn.sigmoid(gate)
    silu = gate * sigmoid
    act_ref[...] = (silu * up).astype(low)
    grad_gate_ref[...] = (grad_act * up * sigmoid * (1.0 + gate * (1.0 - sigmoid))).astype(low)
    grad_up_ref[...] = (grad_act * silu).astype(low)


def feed(rows, dy_rows, w_gate_up, w_down):
    block, width = rows[0].shape
    units = w_down.shape[0]
    tiles = units // TILE
    whole = pl.BlockSpec((N_Z * block, width), lambda j: (0, 0))
    tile = pl.BlockSpec((N_Z * block, TILE), lambda j: (0, j))
    return pl.pallas_call(
        feed_kernel,
        grid=(tiles,),
        in_specs=[pl.BlockSpec(memory_space=pl.ANY)] * (2 * N_Z)
        + [
            pl.BlockSpec((width, TILE), lambda j: (0, j)),
            pl.BlockSpec((width, TILE), lambda j: (0, tiles + j)),
            pl.BlockSpec((TILE, width), lambda j: (j, 0)),
        ],
        out_specs=[tile] * 3 + [whole] * 2,
        out_shape=[jax.ShapeDtypeStruct((N_Z * block, units), low)] * 3
        + [jax.ShapeDtypeStruct((N_Z * block, width), low)] * 2,
        scratch_shapes=[pltpu.SemaphoreType.DMA((2 * N_Z,))],
        compiler_params=pltpu.CompilerParams(vmem_limit_bytes=24 << 20),
        cost_estimate=FILLS,
    )(*rows, *dy_rows, w_gate_up, w_gate_up, w_down)


def unpack_kernel(packed_ref, gate_up_ref, down_ref):
    block = gate_up_ref.shape[0]
    gate_up_ref[...] = packed_ref[0, :block]
    rows, width = down_ref.shape
    for (row, col), (to, lane) in down_chunks(rows, width, gate_up_ref.shape[1]):
        down_ref[row : row + 16, col : col + 512] = packed_ref[
            0, block + to : block + to + 16, lane : lane + 512
        ]


def unpack(packed, block, rows, width):
    fleet, tall, wide = packed.shape
    return pl.pallas_call(
        unpack_kernel,
        grid=(fleet,),
        in_specs=[pl.BlockSpec((1, tall, wide), lambda s: (s, 0, 0))],
        out_specs=[pl.BlockSpec((block, wide), lambda s: (s, 0)), pl.BlockSpec((rows, width), lambda s: (s, 0))],
        out_shape=[
            jax.ShapeDtypeStruct((fleet * block, wide), low),
            jax.ShapeDtypeStruct((fleet * rows, width), low),
        ],
        compiler_params=pltpu.CompilerParams(vmem_limit_bytes=10 << 20),
        cost_estimate=FILLS,
    )(packed)


def feed_back_kernel(gate_ref, up_ref, right_ref, out_ref):
    units = gate_ref.shape[1]
    out_ref[...] = (
        matmul_right_t(gate_ref[...], right_ref[:, :units]) + matmul_right_t(up_ref[...], right_ref[:, units:])
    ).astype(out_ref.dtype)


def feed_back(grad_gate, grad_up, w_gate_up, dtype):
    rows, units = grad_gate.shape
    width = w_gate_up.shape[0]
    whole = pl.BlockSpec((rows, units), lambda j: (0, 0))
    return pl.pallas_call(
        feed_back_kernel,
        grid=(width // 512,),
        in_specs=[whole, whole, pl.BlockSpec((512, 2 * units), lambda j: (j, 0))],
        out_specs=pl.BlockSpec((rows, 512), lambda j: (0, j)),
        out_shape=jax.ShapeDtypeStruct((rows, width), dtype),
        compiler_params=pltpu.CompilerParams(vmem_limit_bytes=20 << 20),
        cost_estimate=FILLS,
    )(grad_gate, grad_up, w_gate_up)


def terms_kernel(
    x0_ref, x1_ref, dy0_ref, dy1_ref, act0_ref, act1_ref, gate0_ref, gate1_ref, up0_ref, up1_ref, out_ref, down
):
    step = pl.program_id(0)
    units = act0_ref.shape[1]
    pad = units // N_FLEET
    block = x0_ref.shape[1]

    @pl.when(step == 0)
    def _():
        for first in range(0, units, TILE):
            at = slice(first, first + TILE)
            down[at] = (
                matmul_left_t(act0_ref[:, at], dy0_ref[...]) + matmul_left_t(act1_ref[:, at], dy1_ref[...])
            ).astype(low)

    for i, (grad0_ref, grad1_ref) in enumerate(((gate0_ref, gate1_ref), (up0_ref, up1_ref))):
        at = slice(i * units, (i + 1) * units)
        term = matmul_left_t(x0_ref[...], grad0_ref[...]) + matmul_left_t(x1_ref[...], grad1_ref[...])
        term = term.astype(low)
        for row in range(0, block, 32):
            for g in range(2):
                out_ref[g, 0, row // 2 : row // 2 + 16, at] = term[row + 16 * g : row + 16 * g + 16]
    rows = down[pl.ds(pl.multiple_of(step * pad, 16), pad)]
    for g in range(2):
        for (row, col), (to, lane) in down_chunks(pad // 2, rows.shape[1], 2 * units):
            first = g * (pad // 2) + row
            out_ref[g, 0, block // 2 + to : block // 2 + to + 16, lane : lane + 512] = rows[
                first : first + 16, col : col + 512
            ]


def down_chunks(rows, width, wide):
    packed = rows * width // wide
    places = [(row, col) for col in range(0, width, 512) for row in range(0, rows, 16)]
    return [(place, (16 * i % packed, 16 * i // packed * 512)) for i, place in enumerate(places)]


def pack_kernel(down_ref, out_ref):
    rows, width = out_ref.shape[0] * out_ref.shape[1] // down_ref.shape[1], down_ref.shape[1]
    held = down_ref[...]
    held = jnp.concatenate([held, jnp.zeros((rows - held.shape[0], width), low)], axis=0)
    for (row, col), (to, lane) in down_chunks(rows, width, out_ref.shape[1]):
        out_ref[to : to + 16, lane : lane + 512] = held[row : row + 16, col : col + 512]


def pack(down, rows, wide):
    return pl.pallas_call(
        pack_kernel,
        out_shape=jax.ShapeDtypeStruct((rows * down.shape[1] // wide, wide), low),
        compiler_params=pltpu.CompilerParams(vmem_limit_bytes=8 << 20),
        cost_estimate=FILLS,
    )(down)


def unpack_down(packed, rows, width):
    parts = {
        place: packed[to : to + 16, lane : lane + 512]
        for place, (to, lane) in down_chunks(rows, width, packed.shape[1])
    }
    return jnp.concatenate(
        [jnp.concatenate([parts[row, col] for col in range(0, width, 512)], axis=1) for row in range(0, rows, 16)],
        axis=0,
    )


def feed_terms(rows, dy_rows, activated, grad_gate, grad_up):
    half, width = rows[0].shape
    units = activated[0].shape[1]
    block = width // N_FLEET
    tall = block // 2 + units // N_FLEET // 2 * width // (2 * units)
    whole = lambda wide: pl.BlockSpec((half, wide), lambda s: (0, 0))
    cut = pl.BlockSpec((half, block), lambda s: (0, s))
    return pl.pallas_call(
        terms_kernel,
        grid=(N_FLEET,),
        in_specs=[cut] * 2 + [whole(width)] * 2 + [whole(units)] * 6,
        out_specs=pl.BlockSpec((2, 1, tall, 2 * units), lambda s: (0, s, 0, 0)),
        out_shape=pltpu.HBM((2, N_FLEET, tall, 2 * units), low),
        scratch_shapes=[pltpu.VMEM((units, width), low)],
        compiler_params=pltpu.CompilerParams(vmem_limit_bytes=28 << 20),
        cost_estimate=pl.CostEstimate(flops=10**10, bytes_accessed=2 * 10**7, transcendentals=0),
    )(*rows, *dy_rows, *activated, *grad_gate, *grad_up)


def down_kernel(left0_ref, left1_ref, right_ref, here_ref, there_ref):
    here_ref[...] = matmul(left0_ref[...], right_ref[...])
    there_ref[...] = matmul(left1_ref[...], right_ref[...]).astype(low)


def down_parts(left, right):
    half, depth = left[0].shape
    width = right.shape[1]
    whole = pl.BlockSpec((half, depth), lambda j: (0, 0))
    tile = pl.BlockSpec((half, 512), lambda j: (0, j))
    return pl.pallas_call(
        down_kernel,
        grid=(width // 512,),
        in_specs=[whole, whole, pl.BlockSpec((depth, 512), lambda j: (0, j))],
        out_specs=[tile, tile],
        out_shape=[jax.ShapeDtypeStruct((half, width), full), jax.ShapeDtypeStruct((half, width), low)],
        compiler_params=pltpu.CompilerParams(vmem_limit_bytes=16 << 20),
        cost_estimate=FILLS,
    )(*left, right)


def segment_numbers(positions, lengths):
    row_ends = jnp.cumsum(lengths)
    return jnp.sum((positions[..., None] >= row_ends).astype(jnp.int32), axis=-1)


def probabilities(query, keys, mask):
    scores = matmul_right_t(query, keys) * SCALE
    scores = jnp.where(mask > 0, scores, -1e30)
    weights = jnp.exp(scores - jnp.max(scores, axis=-1, keepdims=True))
    return weights / jnp.sum(weights, axis=-1, keepdims=True)


def attend_kernel(place, q_ref, k_ref, v_ref, kp_ref, vp_ref, halo_ref, mask_ref, out_ref):
    mask = mask_ref[0]
    wide = q_ref.shape[1]
    at_start = pl.program_id(0) == 0
    for head in range(wide // HEAD):
        at = slice(head * HEAD, (head + 1) * HEAD)
        at_value = slice(wide + head * HEAD, wide + (head + 1) * HEAD)
        keys = jnp.concatenate([jnp.where(at_start, halo_ref[:, at], kp_ref[:, at]), k_ref[:, at]], axis=0)
        values = jnp.concatenate([jnp.where(at_start, halo_ref[:, at_value], vp_ref[:, at]), v_ref[:, at]], axis=0)
        probs = probabilities(q_ref[:, at], keys, mask)
        out_ref[:, at] = matmul(probs.astype(low), values).astype(low)


def block_gradients(query, keys, values, mask, grad_mixed):
    probs = probabilities(query, keys, mask)
    grad_probs = matmul_right_t(grad_mixed, values)
    inner = jnp.sum(probs * grad_probs, axis=-1, keepdims=True)
    return (probs * (grad_probs - inner)).astype(low), probs.astype(low)


def halo_back_kernel(place, q_ref, k_ref, v_ref, halo_ref, mask_ref, gm_ref, back_ref):
    wide = q_ref.shape[1]
    for head in range(wide // HEAD):
        at = slice(head * HEAD, (head + 1) * HEAD)
        at_value = slice(wide + head * HEAD, wide + (head + 1) * HEAD)
        keys = jnp.concatenate([halo_ref[:, at], k_ref[:, at]], axis=0)
        values = jnp.concatenate([halo_ref[:, at_value], v_ref[:, at]], axis=0)
        grad_scores, probs = block_gradients(q_ref[:, at], keys, values, mask_ref[0], gm_ref[:, at])
        back_ref[:, at] = (matmul_left_t(grad_scores, q_ref[:, at])[:WIN] * SCALE).astype(low)
        back_ref[:, at_value] = matmul_left_t(probs, gm_ref[:, at])[:WIN].astype(low)


def halo_back(place, qkv, halo, mask, grad_mixed):
    wide = qkv.shape[1] // 3
    block = lambda column: pl.BlockSpec((BLOCK, wide), lambda s, place: (place[0], column))
    once = pl.BlockSpec((WIN, 2 * wide), lambda s, place: (0, 0))
    return pl.pallas_call(
        halo_back_kernel,
        grid_spec=pltpu.PrefetchScalarGridSpec(
            num_scalar_prefetch=1,
            grid=(1,),
            in_specs=[block(0), block(1), block(2), once]
            + [pl.BlockSpec((1, BLOCK, BLOCK + WIN), lambda s, place: (place[0], 0, 0)), block(0)],
            out_specs=once,
        ),
        out_shape=jax.ShapeDtypeStruct((WIN, 2 * wide), low),
        compiler_params=pltpu.CompilerParams(vmem_limit_bytes=8 << 20),
        cost_estimate=FILLS,
    )(place, qkv, qkv, qkv, halo, mask, grad_mixed)


def attend_back_kernel(
    place, q_ref, k_ref, v_ref, kp_ref, vp_ref, halo_ref, mask_ref, gm_ref, grads_ref, tail_ref, carry
):
    step = pl.program_id(0)
    mask = mask_ref[0]
    wide = q_ref.shape[1]
    at_start = step == N_TEAM - 1

    @pl.when(step == 0)
    def _():
        carry[...] = jnp.zeros_like(carry)

    for head in range(wide // HEAD):
        at = slice(head * HEAD, (head + 1) * HEAD)
        at_value = slice(wide + head * HEAD, wide + (head + 1) * HEAD)
        query = q_ref[:, at]
        keys = jnp.concatenate([jnp.where(at_start, halo_ref[:, at], kp_ref[:, at]), k_ref[:, at]], axis=0)
        values = jnp.concatenate([jnp.where(at_start, halo_ref[:, at_value], vp_ref[:, at]), v_ref[:, at]], axis=0)
        grad_mixed = gm_ref[:, at]
        grad_scores, probs = block_gradients(query, keys, values, mask, grad_mixed)
        grads_ref[:, at] = (matmul(grad_scores, keys) * SCALE).astype(low)
        grad_keys = matmul_left_t(grad_scores, query) * SCALE
        grad_values = matmul_left_t(probs, grad_mixed)
        for here, grad in ((at, grad_keys), (at_value, grad_values)):
            there = slice(wide + here.start, wide + here.stop)
            last = grad[BLOCK:] + carry[:, here]
            grads_ref[: BLOCK - WIN, there] = grad[WIN:BLOCK].astype(low)
            grads_ref[BLOCK - WIN :, there] = last.astype(low)

            @pl.when(step == 0)
            def _(last=last, here=here):
                tail_ref[:, here] = last

            carry[:, here] = grad[:WIN]


def attention_specs(wide, step):
    def block(rows, column, first):
        return pl.BlockSpec((rows, wide), lambda s, place: (place[first + step(s)], column))

    return [
        block(BLOCK, 0, 0),
        block(BLOCK, 1, 0),
        block(BLOCK, 2, 0),
        block(WIN, 1, N_TEAM),
        block(WIN, 2, N_TEAM),
        pl.BlockSpec((WIN, 2 * wide), lambda s, place: (0, 0)),
        pl.BlockSpec((1, BLOCK, BLOCK + WIN), lambda s, place: (place[step(s)], 0, 0)),
    ]


def attend(place, qkv, halo, mask):
    wide = qkv.shape[1] // 3
    return pl.pallas_call(
        attend_kernel,
        grid_spec=pltpu.PrefetchScalarGridSpec(
            num_scalar_prefetch=1,
            grid=(N_TEAM,),
            in_specs=attention_specs(wide, lambda s: s),
            out_specs=pl.BlockSpec((BLOCK, wide), lambda s, place: (place[s], 0)),
        ),
        out_shape=jax.ShapeDtypeStruct((N_TEAM * BLOCK, wide), low),
        compiler_params=pltpu.CompilerParams(vmem_limit_bytes=8 << 20),
        cost_estimate=FILLS,
    )(place, qkv, qkv, qkv, qkv, qkv, halo, mask)


def attend_back(place, qkv, halo, mask, grad_mixed):
    wide = qkv.shape[1] // 3
    step = lambda s: N_TEAM - 1 - s
    by_block = lambda width: pl.BlockSpec((BLOCK, width), lambda s, place: (place[step(s)], 0))
    once = pl.BlockSpec((WIN, 2 * wide), lambda s, place: (0, 0))
    return pl.pallas_call(
        attend_back_kernel,
        grid_spec=pltpu.PrefetchScalarGridSpec(
            num_scalar_prefetch=1,
            grid=(N_TEAM,),
            in_specs=attention_specs(wide, step) + [by_block(wide)],
            out_specs=[by_block(3 * wide), once],
            scratch_shapes=[pltpu.VMEM((WIN, 2 * wide), full)],
        ),
        out_shape=[
            jax.ShapeDtypeStruct((N_TEAM * BLOCK, 3 * wide), low),
            jax.ShapeDtypeStruct((WIN, 2 * wide), full),
        ],
        compiler_params=pltpu.CompilerParams(vmem_limit_bytes=8 << 20),
        cost_estimate=FILLS,
    )(place, qkv, qkv, qkv, qkv, qkv, halo, mask, grad_mixed)


def attn_terms_kernel(normed_ref, grad_ref, mixed_ref, hidden0_ref, hidden1_ref, out_ref, out_term):
    step = pl.program_id(0)
    half = hidden0_ref.shape[0]
    wide, deep = mixed_ref.shape[1], grad_ref.shape[1]
    rows = wide // N_FLEET

    @pl.when(step == 0)
    def _():
        out_term[...] = (
            matmul_left_t(mixed_ref[:half], hidden0_ref[...]) + matmul_left_t(mixed_ref[half:], hidden1_ref[...])
        ).astype(low)

    out_ref[:, :deep] = matmul_left_t(normed_ref[...], grad_ref[...]).astype(low)
    part = out_term[pl.ds(pl.multiple_of(step * rows, 32), rows)]
    for t in range(N_TEAM):
        out_ref[rows * t : rows * (t + 1), deep:] = part[:, wide * t : wide * (t + 1)]


def attn_terms(normed, grad_qkv, mixed, hidden_low):
    rows, width = normed.shape
    half, wide, deep = rows // 2, mixed.shape[1], grad_qkv.shape[1]
    block = width // N_FLEET
    whole = lambda shape: pl.BlockSpec(shape, lambda s: (0, 0))
    return pl.pallas_call(
        attn_terms_kernel,
        grid=(N_FLEET,),
        in_specs=[pl.BlockSpec((rows, block), lambda s: (0, s)), whole((rows, deep)), whole((rows, wide))]
        + [whole((half, width))] * 2,
        out_specs=pl.BlockSpec((block, deep + wide), lambda s: (s, 0)),
        out_shape=pltpu.HBM((width, deep + wide), low),
        scratch_shapes=[pltpu.VMEM((wide, width), low)],
        compiler_params=pltpu.CompilerParams(vmem_limit_bytes=18 << 20),
        cost_estimate=FILLS,
    )(normed, grad_qkv, mixed, *hidden_low)


def summed(refs, at):
    return refs[0][at] + sum(ref[at].astype(full) for ref in refs[1:])


def own_rows(kernel, out_types, *operands):
    shape = operands[0].shape
    n = len(operands)

    def whole(*refs):
        sources, outs, held, arrived = refs[:n], refs[n:-n - 1], refs[-n - 1 : -1], refs[-1]
        copies = [pltpu.make_async_copy(sources[i], held[i], arrived.at[i]) for i in range(n)]
        for copy in copies:
            copy.start()
        for copy in copies:
            copy.wait()
        for first in range(0, shape[0], 16):
            kernel(slice(first, first + 16), (*held, *outs))

    return pl.pallas_call(
        whole,
        in_specs=[pl.BlockSpec(memory_space=pl.ANY)] * n,
        out_shape=[jax.ShapeDtypeStruct(shape, dtype) for dtype in out_types],
        scratch_shapes=[pltpu.VMEM(operand.shape, operand.dtype) for operand in operands]
        + [pltpu.SemaphoreType.DMA((n,))],
        compiler_params=pltpu.CompilerParams(vmem_limit_bytes=12 << 20),
        cost_estimate=FILLS,
    )(*operands)


def hidden_kernel(at, refs):
    *parts, x_ref, gain_ref, hidden_ref, again_ref = refs
    hidden = x_ref[at].astype(full) + summed(parts, at)
    hidden_ref[at] = hidden
    again_ref[at] = (hidden * inverse_rms(hidden) * gain_ref[...]).astype(low)


def norm_backward(grad_normed, inputs, gain):
    scale_rows = inverse_rms(inputs)
    weighted = grad_normed * gain
    return scale_rows * weighted - inputs * scale_rows**3 * jnp.mean(
        weighted * inputs, axis=-1, keepdims=True
    )


def grad_hidden_kernel(at, refs):
    *parts, hidden_ref, dy_ref, gain_ref, grad_ref, low_ref = refs
    grad = dy_ref[at].astype(full) + norm_backward(summed(parts, at), hidden_ref[at], gain_ref[...])
    grad_ref[at] = grad
    low_ref[at] = grad.astype(low)


def input_grad_kernel(at, refs):
    *parts, x_ref, grad_ref, gain_ref, out_ref = refs
    out_ref[at] = grad_ref[at] + norm_backward(summed(parts, at), x_ref[at].astype(full), gain_ref[...])


def outputs_kernel(at, refs):
    *parts, hidden_ref, out_ref = refs
    out_ref[at] = (hidden_ref[at] + summed(parts, at)).astype(low)


def feed_owner_kernel(unit_rows, group, here_ref, there_ref, w_gate_ref, w_up_ref, gain_ref, gate_ref, up_ref, grad_ref):
    rows = here_ref.shape[1]
    units = here_ref.shape[2] // 2
    pad = units // N_FLEET
    first = group[0] == 0
    for t in range(N_TEAM):
        here, there = here_ref[t], there_ref[t]
        block = jnp.concatenate([jnp.where(first, here, there), jnp.where(first, there, here)], axis=0).astype(full)
        for i, out_ref in enumerate((gate_ref, up_ref)):
            for f in range(N_FLEET):
                at = i * units + f * pad
                to = (f * N_TEAM + t) * unit_rows
                out_ref[:, to : to + unit_rows] = block[:, at : at + unit_rows]
    for row in range(0, 2 * rows, 16):
        at = slice(row, row + 16)
        total = w_gate_ref[at].astype(full) * gate_ref[at] + w_up_ref[at].astype(full) * up_ref[at]
        grad_ref[at] = jnp.sum(total, axis=1, keepdims=True) / gain_ref[at].astype(full)


def feed_owner(group, here, there, w_gate, w_up, gain):
    shard, wide = w_gate.shape
    vmem = pl.BlockSpec(memory_space=pltpu.VMEM)
    return pl.pallas_call(
        functools.partial(feed_owner_kernel, wide // (N_FLEET * N_TEAM)),
        in_specs=[pl.BlockSpec(memory_space=pltpu.SMEM)] + [vmem] * 5,
        out_specs=[vmem] * 3,
        out_shape=[jax.ShapeDtypeStruct((shard, wide), full)] * 2 + [jax.ShapeDtypeStruct((shard, 1), full)],
        compiler_params=pltpu.CompilerParams(vmem_limit_bytes=10 << 20),
        cost_estimate=FILLS,
    )(group, here, there, w_gate, w_up, gain[:, None])


def attn_owner_kernel(
    sums_ref, out0_ref, out1_ref, w_query_ref, w_key_ref, w_value_ref, gain_ref,
    query_ref, key_ref, value_ref, out_ref, grad_ref,
):
    wide = sums_ref.shape[2] // 3
    weights = (w_query_ref, w_key_ref, w_value_ref)
    total = jnp.zeros((query_ref.shape[0], wide), full)
    for t in range(N_TEAM):
        to = slice(t * wide, (t + 1) * wide)
        block = sums_ref[t].astype(full) + sums_ref[N_TEAM + t].astype(full)
        for i, grad in enumerate((query_ref, key_ref, value_ref)):
            part = block[:, i * wide : (i + 1) * wide]
            grad[:, to] = part
            total += part * weights[i][:, to].astype(full)
        out_ref[:, to] = out0_ref[t].astype(full) + out1_ref[t].astype(full)
    grad_ref[...] = jnp.sum(total, axis=1, keepdims=True) / gain_ref[...].astype(full)


def attn_owner(sums, out_sums, w_query, w_key, w_value, gain):
    grad = jax.ShapeDtypeStruct(w_query.shape, full)
    return pl.pallas_call(
        attn_owner_kernel,
        out_shape=[grad] * 4 + [jax.ShapeDtypeStruct((w_query.shape[0], 1), full)],
        compiler_params=pltpu.CompilerParams(vmem_limit_bytes=8 << 20),
        cost_estimate=FILLS,
    )(sums, *out_sums, w_query, w_key, w_value, gain[:, None])


def body(
    tokens, lengths, norm_gain, w_query, w_key, w_value, w_out, mlp_gain, w_gate, w_up, w_down, cotangent
):
    rows, width = tokens.shape
    shard = w_query.shape[0]
    team_wide = width // N_TEAM
    unit_rows = w_down.shape[0]
    unit_pad = -(-unit_rows // 32) * 32
    units = N_FLEET * unit_pad
    x, yl, z, c = [lax.axis_index(axis) for axis in ("x", "yl", "z", "c")]
    fleet = lax.axis_index(FLEET)

    order = jnp.arange(N_TEAM, dtype=jnp.int32)
    spot = (jnp.bitwise_xor(order % N_C, c) * N_Z + (order // N_C - z) % N_Z).astype(jnp.int32)
    before = jnp.concatenate([jnp.zeros((1,), jnp.int32), 2 * spot[:-1] + 1])
    place = jnp.concatenate([spot, before])
    last_spot = (1 - c) * N_Z + N_Z - 1 - z
    last_at = last_spot * BLOCK + BLOCK - WIN
    kept = jnp.arange(N_TEAM, dtype=jnp.int32)
    kept_block = N_C * ((kept % N_Z + z) % N_Z) + jnp.bitwise_xor(kept // N_Z, c)
    first_pos = (fleet * N_TEAM + kept_block) * BLOCK
    query_pos = first_pos[:, None] + jnp.arange(BLOCK, dtype=jnp.int32)
    key_pos = first_pos[:, None] - WIN + jnp.arange(BLOCK + WIN, dtype=jnp.int32)
    query_segs = segment_numbers(query_pos, lengths[0])
    key_segs = jnp.where(key_pos >= 0, segment_numbers(key_pos, lengths[0]), -1)
    distance = query_pos[:, :, None] - key_pos[:, None, :]
    mask = (distance >= 0) & (distance < WIN) & (query_segs[:, :, None] == key_segs[:, None, :])
    mask = mask.astype(full)

    gains = jnp.concatenate([norm_gain[:, None], mlp_gain[:, None], jnp.zeros((shard, 126), low)], axis=1)
    out_there = swapped(w_out)
    x_mine = [tokens, from_ahead(tokens, "z", 1), None, from_ahead(tokens, "z", 3)]
    cut = attn_cut(w_query, w_key, w_value, gains)
    cut = lax.all_to_all(cut, TEAM, 0, 0, tiled=True).reshape(N_TEAM * shard, -1)
    out_cut = out_there.reshape(shard, N_TEAM, team_wide).transpose(1, 0, 2)
    out_cut = out_cut.reshape(N_TEAM * shard, team_wide)
    cut, out_cut, x_mine, w_gate_later, dy = lax.optimization_barrier((cut, out_cut, x_mine, w_gate, cotangent))
    at_out = cut.shape[1]
    attn_piece = jnp.concatenate([cut, out_cut], axis=1)
    along_y = lambda value, by: from_ahead(value, ("g", "yl"), by)
    other = lambda block: from_ahead(block, "c", 1)
    attn = lax.all_to_all(jnp.broadcast_to(attn_piece, (N_X, *attn_piece.shape)), "x", 0, 0, tiled=True)
    attn = attn.reshape(N_X * N_TEAM * shard, -1)
    x_mine[2] = from_ahead(x_mine[0], "z", 2)
    x_other = [other(x_mine[0]), other(x_mine[1]), None, other(x_mine[3])]
    gate_up = feed_cut(w_gate_later, w_up, unit_rows, units)
    down_piece = pack(w_down, unit_pad, 2 * units)
    attn, x_mine, x_other, dy, gate_up, down_piece, place, mask = lax.optimization_barrier(
        (attn, x_mine, x_other, dy, gate_up, down_piece, place, mask)
    )
    x_other[2] = other(x_mine[2])
    x_blocks = x_mine + x_other
    halo = along_line(lax.select_n(last_spot, *[block[BLOCK - WIN :] for block in x_blocks]), 1)
    gate_up_piece = lax.all_to_all(gate_up, TEAM, 0, 0, tiled=True).reshape(N_TEAM * shard, -1)
    attn_there = along_y(attn[: width // 4], 1), along_y(attn[width // 4 :], -1)
    dy_mine = [dy, from_ahead(dy, "z", 1), None, from_ahead(dy, "z", 3)]
    attn, attn_there, x_blocks, halo, dy_mine, gate_up_piece = lax.optimization_barrier(
        (attn, attn_there, x_blocks, halo, dy_mine, gate_up_piece)
    )
    feed_piece = jnp.concatenate([gate_up_piece, down_piece], axis=0)
    w_feed = lax.all_gather(feed_piece, FLEET, axis=0, tiled=False)
    dy_mine[2] = from_ahead(dy_mine[0], "z", 2)

    half = N_Z * BLOCK
    whole = jnp.zeros((width, attn.shape[1]), low)
    whole = lax.dynamic_update_slice(whole, attn, (yl * (width // 2), 0))
    whole = lax.dynamic_update_slice(whole, attn_there[0], ((1 - yl) * (width // 2), 0))
    attn = lax.dynamic_update_slice(whole, attn_there[1], ((1 - yl) * (width // 2) + width // 4, 0))
    w_qkv = attn[:, : 3 * team_wide]
    w_out_team = attn[:, at_out:].reshape(N_FLEET, N_TEAM, shard, team_wide)
    w_out_team = w_out_team.transpose(0, 2, 1, 3).reshape(N_FLEET * shard, width)
    normed, gain_rows = normalised(x_blocks, attn[:, 3 * team_wide : at_out])
    gain_one, gain_two = gain_rows[:1], gain_rows[1:2]
    qkv = matmul(normed, w_qkv).astype(low)
    qkv, dy_mine = lax.optimization_barrier((qkv, dy_mine))
    halo = halo.astype(full)
    halo = matmul((halo * inverse_rms(halo) * gain_one).astype(low), w_qkv[:, team_wide:]).astype(low)
    mixed = attend(place, qkv, halo, mask)
    halves = lambda rows: (rows[:half], rows[half : 2 * half])
    hidden_blocks = core_sum(halves(mixed), lambda rows: matmul(rows, w_out_team))
    hidden_blocks, dy_mine = lax.optimization_barrier((hidden_blocks, dy_mine))
    dy_other = [other(block) for block in dy_mine]
    hidden_parts, dy_mine, dy_other = lax.optimization_barrier((z_send(hidden_blocks), dy_mine, dy_other))

    hidden, again = own_rows(hidden_kernel, (full, low), *hidden_parts, tokens, gain_two)
    again = z_gather(again)
    again_other = [other(block) for block in again[:2]] + [None, other(again[3])]
    again, again_other[:2], again_other[3] = lax.optimization_barrier((again, again_other[:2], again_other[3]))
    again_other[2] = other(again[2])
    w_gate_up, w_down_team = unpack(w_feed, N_TEAM * shard, unit_pad, width)
    act_mine, gate_mine, up_mine, x_mine, dy_mine = feed(again, dy_mine, w_gate_up, w_down_team)
    act_other, gate_other, up_other, x_other, dy_other = feed(again_other, dy_other, w_gate_up, w_down_team)
    there = feed_back(gate_other, up_other, w_gate_up, low)
    again_blocks = core_blocks(feed_back(gate_mine, up_mine, w_gate_up, full), there)
    activated, grad_gate, grad_up = (act_mine, act_other), (gate_mine, gate_other), (up_mine, up_other)
    again_blocks, activated, grad_gate, grad_up = lax.optimization_barrier(
        (again_blocks, activated, grad_gate, grad_up)
    )
    mlp_term = feed_terms((x_mine, x_other), (dy_mine, dy_other), activated, grad_gate, grad_up)
    again_parts = z_send(again_blocks)
    mlp_term, again_parts[1], again_parts[3] = lax.optimization_barrier((mlp_term, again_parts[1], again_parts[3]))
    mlp_sum = lax.psum_scatter(
        mlp_term.reshape(-1, 2 * units), ("g", *FLEET), scatter_dimension=0, tiled=True
    )

    grad_hidden, hidden_low = own_rows(grad_hidden_kernel, (full, low), *again_parts, hidden, cotangent, gain_two)
    output_parts = down_parts(activated, w_down_team)
    hidden_low, output_parts = lax.optimization_barrier((z_gather(hidden_low), output_parts))
    hidden_low = [join(hidden_low)]
    hidden_low.append(other(hidden_low[0]))
    output_blocks = core_blocks(*output_parts)

    grad_mixed = [matmul_right_t(rows, w_out_team).astype(low) for rows in hidden_low]
    grad_mixed = jnp.concatenate(grad_mixed, axis=0)
    back = halo_back(place, qkv, halo, mask, grad_mixed)
    grad_qkv, tail = attend_back(place, qkv, halo, mask, grad_mixed)
    tail = tail + along_line(back, -1).astype(full)
    grad_qkv = lax.dynamic_update_slice(grad_qkv, tail.astype(low), (last_at, team_wide))
    attn_term = attn_terms(normed, grad_qkv, mixed, hidden_low)
    attn_term, grad_qkv, output_parts = lax.optimization_barrier((attn_term, grad_qkv, z_send(output_blocks)))
    attn_sum = lax.psum_scatter(attn_term, FLEET, scatter_dimension=0, tiled=True)
    (outputs,) = own_rows(outputs_kernel, (low,), *output_parts, hidden)
    normed_blocks = core_sum(halves(grad_qkv), lambda rows: matmul_right_t(rows, w_qkv))

    down_sum = unpack_down(mlp_sum[N_TEAM * shard // 2 :], unit_pad // 2, width)
    gate_up_sum = mlp_sum[: N_TEAM * shard // 2].reshape(N_TEAM, shard // 2, 2 * units)
    gate_up_sum = lax.all_to_all(gate_up_sum, TEAM, 0, 0, tiled=True)
    normed_blocks, gate_up_sum, down_sum = lax.optimization_barrier((normed_blocks, gate_up_sum, down_sum))
    gate_up_there, down_there = from_ahead(gate_up_sum, "g", 1), from_ahead(down_sum, "g", 1)
    normed_parts, attn_sum, outputs, gate_up_there, down_there = lax.optimization_barrier(
        (z_send(normed_blocks), attn_sum, outputs, gate_up_there, down_there)
    )
    (input_grad,) = own_rows(input_grad_kernel, (full,), *normed_parts, tokens, grad_hidden, gain_one)
    qkv_sum = attn_sum[:, : 3 * team_wide].reshape(N_TEAM, shard, 3 * team_wide)
    qkv_sum = lax.all_to_all(jnp.concatenate([qkv_sum, qkv_sum], axis=0), ("g", *TEAM), 0, 0, tiled=True)
    out_sum = attn_sum[:, 3 * team_wide :].reshape(N_TEAM, shard, team_wide)
    group = lax.axis_index("g")
    gate_grad, up_grad, mlp_gain_grad = feed_owner(
        group[None].astype(jnp.int32), gate_up_sum, gate_up_there, w_gate, w_up, mlp_gain
    )
    qkv_sum, out_sums, input_grad, gate_grad = lax.optimization_barrier(
        (qkv_sum, (swapped(out_sum), swapped(out_sum, 1)), input_grad, gate_grad)
    )
    query_grad, key_grad, value_grad, out_grad, gain_grad = attn_owner(
        qkv_sum, out_sums, w_query, w_key, w_value, norm_gain
    )
    first, second = jnp.where(group == 0, down_sum, down_there), jnp.where(group == 0, down_there, down_sum)
    down_grad = jnp.concatenate([first, second], axis=0)[:unit_rows].astype(full)
    return (
        outputs,
        input_grad,
        gain_grad[:, 0],
        query_grad,
        key_grad,
        value_grad,
        out_grad,
        mlp_gain_grad[:, 0],
        gate_grad,
        up_grad,
        down_grad,
    )


def solution(mesh):
    fine = Mesh(mesh.devices.reshape(2, 2, 4, 4, 2), ALL)
    return jax.shard_map(
        body,
        mesh=fine,
        in_specs=(
            P(ALL, None),
            P("g", None),
            P(SEQ),
            P(SEQ, None),
            P(SEQ, None),
            P(SEQ, None),
            P(SEQ, None),
            P(SEQ),
            P(SEQ, None),
            P(SEQ, None),
            P(SEQ, None),
            P(ALL, None),
        ),
        out_specs=(
            P(ALL, None),
            P(ALL, None),
            P(SEQ),
            P(SEQ, None),
            P(SEQ, None),
            P(SEQ, None),
            P(SEQ, None),
            P(SEQ),
            P(SEQ, None),
            P(SEQ, None),
            P(SEQ, None),
        ),
        check_vma=False,
    )
```

```python
import functools

import jax
import jax.numpy as jnp
from jax import lax
from jax.experimental import pallas as pl
from jax.experimental.pallas import tpu as pltpu
from jax.sharding import Mesh
from jax.sharding import PartitionSpec as P

FILLS = pl.CostEstimate(flops=1, bytes_accessed=1, transcendentals=0)
HEAD = 128
WIN = 64
BLOCK = 128
epsilon = 1e-06

TEAM = ("z", "c")
FLEET = ("yl", "x")
SEQ = ("yl", "x", "z", "c")
ALL = ("g", "yl", "x", "z", "c")
N_X, N_Z, N_C, N_TEAM, N_FLEET = 4, 4, 2, 8, 8
SCALE = HEAD ** (-0.5)
low = jnp.bfloat16
full = jnp.float32


def from_ahead(value, axis, by):
    n = lax.axis_size(axis)
    return lax.ppermute(value, axis, [((i + by) % n, i) for i in range(n)])


def along_line(value, by):
    return lax.ppermute(
        value, FLEET, [(i, i + by) for i in range(N_FLEET) if 0 <= i + by < N_FLEET]
    )


def swapped(value, across=0):
    n = N_FLEET * N_TEAM
    pairs = [(N_TEAM * f + t, N_TEAM * t + f) for f in range(N_FLEET) for t in range(N_TEAM)]
    return lax.ppermute(value, ALL, [(g * n + a, (g ^ across) * n + b) for g in range(2) for a, b in pairs])


def z_gather(value):
    return [value] + [from_ahead(value, "z", k) for k in (1, 2, 3)]


def z_send(blocks):
    return [blocks[0]] + [from_ahead(blocks[k], "z", -k) for k in (1, 2, 3)]


def core_sum(left, right):
    there = right(left[1]).astype(low)
    return core_blocks(right(left[0]), there)


def inverse_rms(values):
    return lax.rsqrt(jnp.mean(values * values, axis=-1, keepdims=True) + epsilon)


def matmul(left, right):
    return jnp.dot(left, right, preferred_element_type=full)


def matmul_left_t(left, right):
    return lax.dot_general(left, right, (((0,), (0,)), ((), ())), preferred_element_type=full)


def matmul_right_t(left, right):
    return lax.dot_general(left, right, (((1,), (1,)), ((), ())), preferred_element_type=full)


def attn_cut_kernel(gain_ref, mlp_gain_ref, *refs):
    sources, out_ref, held, rows, arrived = refs[:3], refs[3], refs[4:7], refs[7], refs[8]
    copies = [pltpu.make_async_copy(sources[i], held[i], arrived.at[i]) for i in range(3)]
    for copy in copies:
        copy.start()
    shard, width = sources[0].shape
    wide = width // N_TEAM
    rows[...] = jnp.zeros_like(rows)
    rows[0:1, :shard] = gain_ref[...].astype(full)
    rows[1:2, :shard] = mlp_gain_ref[...].astype(full)
    gains = rows[...].T[:shard].astype(low)
    out_ref[:, :, 3 * wide :] = jnp.zeros((N_TEAM, shard, out_ref.shape[2] - 3 * wide), low)
    for copy in copies:
        copy.wait()
    for t in range(N_TEAM):
        for i, ref in enumerate(held):
            out_ref[t, :, i * wide : (i + 1) * wide] = ref[:, t * wide : (t + 1) * wide]
        out_ref[t, :, 3 * wide : 3 * wide + 8] = gains


def attn_cut(w_query, w_key, w_value, norm_gain, mlp_gain):
    shard, width = w_query.shape
    vmem = pl.BlockSpec(memory_space=pltpu.VMEM)
    return pl.pallas_call(
        attn_cut_kernel,
        in_specs=[vmem] * 2 + [pl.BlockSpec(memory_space=pl.ANY)] * 3,
        out_shape=jax.ShapeDtypeStruct((N_TEAM, shard, 3 * width // N_TEAM + 128), low),
        scratch_shapes=[pltpu.VMEM((shard, width), low)] * 3
        + [pltpu.VMEM((8, 128), full), pltpu.SemaphoreType.DMA((3,))],
        compiler_params=pltpu.CompilerParams(vmem_limit_bytes=8 << 20),
    )(norm_gain[None], mlp_gain[None], w_query, w_key, w_value)


def assemble_kernel(at, own_ref, low_ref, high_ref, *refs):
    *pair_refs, qkv_ref, out_ref, gain_ref = refs
    yl, x = at[0], at[1]
    rows = own_ref.shape[0]
    qkv_ref[pl.ds(pl.multiple_of(yl * rows, 256), rows)] = own_ref[...]
    there = (1 - yl) * rows
    qkv_ref[pl.ds(pl.multiple_of(there, 256), rows // 2)] = low_ref[...]
    qkv_ref[pl.ds(pl.multiple_of(there + rows // 2, 256), rows // 2)] = high_ref[...]
    block, wide = pair_refs[0].shape[0] // 2, pair_refs[0].shape[1] - 128
    shard = block // N_TEAM
    for k, pair_ref in enumerate(pair_refs):
        for side in range(2):
            fleet = (yl + side) % 2 * N_X + (x + k) % N_X
            piece = slice(side * block, (side + 1) * block)
            gains = pair_ref[piece, :128].astype(full).T[: gain_ref.shape[0]]
            gain_ref[:, pl.ds(pl.multiple_of(fleet * block, 256), block)] = gains
            to = pl.ds(pl.multiple_of(fleet * shard, 32), shard)
            for t in range(N_TEAM):
                first = side * block + t * shard
                out_ref[to, t * wide : (t + 1) * wide] = pair_ref[first : first + shard, 128:]


def assemble(at, own, there, pairs):
    width, wide = 2 * own.shape[0], pairs[0].shape[1] - 128
    vmem = pl.BlockSpec(memory_space=pltpu.VMEM)
    return pl.pallas_call(
        assemble_kernel,
        in_specs=[pl.BlockSpec(memory_space=pltpu.SMEM)] + [vmem] * (3 + N_X),
        out_specs=[vmem] * 3,
        out_shape=[
            jax.ShapeDtypeStruct((width, own.shape[1]), low),
            jax.ShapeDtypeStruct((wide, width), low),
            jax.ShapeDtypeStruct((8, width), full),
        ],
        compiler_params=pltpu.CompilerParams(vmem_limit_bytes=16 << 20),
        cost_estimate=FILLS,
    )(at, own, *there, *pairs)


def feed_cut_kernel(unit_rows, gate_ref, up_ref, out_ref):
    units = out_ref.shape[2] // 2
    pad = units // N_FLEET
    out_ref[...] = jnp.zeros(out_ref.shape, low)
    for t in range(N_TEAM):
        for i, ref in enumerate((gate_ref, up_ref)):
            for f in range(N_FLEET):
                at = i * units + f * pad
                first = (f * N_TEAM + t) * unit_rows
                out_ref[t, :, at : at + unit_rows] = ref[:, first : first + unit_rows]


def feed_cut(w_gate, w_up, unit_rows, units):
    return pl.pallas_call(
        functools.partial(feed_cut_kernel, unit_rows),
        out_shape=jax.ShapeDtypeStruct((N_TEAM, w_gate.shape[0], 2 * units), low),
        compiler_params=pltpu.CompilerParams(vmem_limit_bytes=8 << 20),
        cost_estimate=FILLS,
    )(w_gate, w_up)


def join_kernel(*refs):
    rows = refs[0].shape[0]
    for i, ref in enumerate(refs[:-1]):
        refs[-1][i * rows : (i + 1) * rows] = ref[...]


def join(blocks):
    rows, width = blocks[0].shape
    return pl.pallas_call(
        join_kernel,
        out_shape=jax.ShapeDtypeStruct((len(blocks) * rows, width), low),
        compiler_params=pltpu.CompilerParams(vmem_limit_bytes=8 << 20),
        cost_estimate=FILLS,
    )(*blocks)


def pair_kernel(here_ref, there_ref, own_ref, *block_refs):
    rows = own_ref.shape[0]
    for i, ref in enumerate((own_ref, *block_refs)):
        at = slice(i * rows, (i + 1) * rows)
        ref[...] = (here_ref[at] + there_ref[at].astype(full)).astype(ref.dtype)


def core_blocks(here, there):
    rows, width = here.shape[0] // N_Z, here.shape[1]
    return pl.pallas_call(
        pair_kernel,
        out_shape=[jax.ShapeDtypeStruct((rows, width), full)] + [jax.ShapeDtypeStruct((rows, width), low)] * 3,
        compiler_params=pltpu.CompilerParams(vmem_limit_bytes=12 << 20),
        cost_estimate=FILLS,
    )(here, from_ahead(there, "c", 1))


def norm_kernel(*refs):
    *block_refs, gain_ref, out_ref = refs
    gain = gain_ref[:1]
    at = 0
    for ref in block_refs:
        for first in range(0, ref.shape[0], 16):
            values = ref[first : first + 16].astype(full)
            out_ref[at + first : at + first + 16] = (values * inverse_rms(values) * gain).astype(low)
        at += ref.shape[0]


def normalised(blocks, gain_rows):
    rows = sum(block.shape[0] for block in blocks)
    return pl.pallas_call(
        norm_kernel,
        out_shape=jax.ShapeDtypeStruct((rows, blocks[0].shape[1]), low),
        compiler_params=pltpu.CompilerParams(vmem_limit_bytes=14 << 20),
        cost_estimate=FILLS,
    )(*blocks, gain_rows)


TILE = 256


def feed_kernel(*refs):
    sources = refs[: 2 * N_Z]
    gate_ref, up_ref, down_ref, act_ref, grad_gate_ref, grad_up_ref, x_ref, dy_ref, arrived = refs[2 * N_Z :]
    rows = sources[0].shape[0]

    @pl.when(pl.program_id(0) == 0)
    def _():
        places = [ref.at[pl.ds(i * rows, rows)] for ref in (x_ref, dy_ref) for i in range(N_Z)]
        copies = [pltpu.make_async_copy(sources[i], places[i], arrived.at[i]) for i in range(2 * N_Z)]
        for copy in copies:
            copy.start()
        for copy in copies:
            copy.wait()

    gate = matmul(x_ref[...], gate_ref[...])
    up = matmul(x_ref[...], up_ref[...])
    grad_act = matmul_right_t(dy_ref[...], down_ref[...])
    sigmoid = jax.nn.sigmoid(gate)
    silu = gate * sigmoid
    act_ref[...] = (silu * up).astype(low)
    grad_gate_ref[...] = (grad_act * up * sigmoid * (1.0 + gate * (1.0 - sigmoid))).astype(low)
    grad_up_ref[...] = (grad_act * silu).astype(low)


def feed(rows, dy_rows, w_gate_up, w_down):
    block, width = rows[0].shape
    units = w_down.shape[0]
    tiles = units // TILE
    whole = pl.BlockSpec((N_Z * block, width), lambda j: (0, 0))
    tile = pl.BlockSpec((N_Z * block, TILE), lambda j: (0, j))
    return pl.pallas_call(
        feed_kernel,
        grid=(tiles,),
        in_specs=[pl.BlockSpec(memory_space=pl.ANY)] * (2 * N_Z)
        + [
            pl.BlockSpec((width, TILE), lambda j: (0, j)),
            pl.BlockSpec((width, TILE), lambda j: (0, tiles + j)),
            pl.BlockSpec((TILE, width), lambda j: (j, 0)),
        ],
        out_specs=[tile] * 3 + [whole] * 2,
        out_shape=[jax.ShapeDtypeStruct((N_Z * block, units), low)] * 3
        + [jax.ShapeDtypeStruct((N_Z * block, width), low)] * 2,
        scratch_shapes=[pltpu.SemaphoreType.DMA((2 * N_Z,))],
        compiler_params=pltpu.CompilerParams(vmem_limit_bytes=24 << 20),
        cost_estimate=FILLS,
    )(*rows, *dy_rows, w_gate_up, w_gate_up, w_down)


def unpack_kernel(packed_ref, gate_up_ref, down_ref):
    block = gate_up_ref.shape[0]
    gate_up_ref[...] = packed_ref[0, :block]
    rows, width = down_ref.shape
    for (row, col), (to, lane) in down_chunks(rows, width, gate_up_ref.shape[1]):
        down_ref[row : row + 16, col : col + 512] = packed_ref[
            0, block + to : block + to + 16, lane : lane + 512
        ]


def unpack(packed, block, rows, width):
    fleet, tall, wide = packed.shape
    return pl.pallas_call(
        unpack_kernel,
        grid=(fleet,),
        in_specs=[pl.BlockSpec((1, tall, wide), lambda s: (s, 0, 0))],
        out_specs=[pl.BlockSpec((block, wide), lambda s: (s, 0)), pl.BlockSpec((rows, width), lambda s: (s, 0))],
        out_shape=[
            jax.ShapeDtypeStruct((fleet * block, wide), low),
            jax.ShapeDtypeStruct((fleet * rows, width), low),
        ],
        compiler_params=pltpu.CompilerParams(vmem_limit_bytes=10 << 20),
        cost_estimate=FILLS,
    )(packed)


def feed_back_kernel(gate_ref, up_ref, right_ref, out_ref):
    units = gate_ref.shape[1]
    out_ref[...] = (
        matmul_right_t(gate_ref[...], right_ref[:, :units]) + matmul_right_t(up_ref[...], right_ref[:, units:])
    ).astype(out_ref.dtype)


def feed_back(grad_gate, grad_up, w_gate_up, dtype):
    rows, units = grad_gate.shape
    width = w_gate_up.shape[0]
    whole = pl.BlockSpec((rows, units), lambda j: (0, 0))
    return pl.pallas_call(
        feed_back_kernel,
        grid=(width // 512,),
        in_specs=[whole, whole, pl.BlockSpec((512, 2 * units), lambda j: (j, 0))],
        out_specs=pl.BlockSpec((rows, 512), lambda j: (0, j)),
        out_shape=jax.ShapeDtypeStruct((rows, width), dtype),
        compiler_params=pltpu.CompilerParams(vmem_limit_bytes=20 << 20),
        cost_estimate=FILLS,
    )(grad_gate, grad_up, w_gate_up)


def terms_kernel(
    x0_ref, x1_ref, dy0_ref, dy1_ref, act0_ref, act1_ref, gate0_ref, gate1_ref, up0_ref, up1_ref, out_ref, down
):
    step = pl.program_id(0)
    units = act0_ref.shape[1]
    pad = units // N_FLEET
    block = x0_ref.shape[1]

    @pl.when(step == 0)
    def _():
        for first in range(0, units, TILE):
            at = slice(first, first + TILE)
            down[at] = (
                matmul_left_t(act0_ref[:, at], dy0_ref[...]) + matmul_left_t(act1_ref[:, at], dy1_ref[...])
            ).astype(low)

    for i, (grad0_ref, grad1_ref) in enumerate(((gate0_ref, gate1_ref), (up0_ref, up1_ref))):
        at = slice(i * units, (i + 1) * units)
        term = matmul_left_t(x0_ref[...], grad0_ref[...]) + matmul_left_t(x1_ref[...], grad1_ref[...])
        term = term.astype(low)
        for row in range(0, block, 32):
            for g in range(2):
                out_ref[g, 0, row // 2 : row // 2 + 16, at] = term[row + 16 * g : row + 16 * g + 16]
    rows = down[pl.ds(pl.multiple_of(step * pad, 16), pad)]
    for g in range(2):
        for (row, col), (to, lane) in down_chunks(pad // 2, rows.shape[1], 2 * units):
            first = g * (pad // 2) + row
            out_ref[g, 0, block // 2 + to : block // 2 + to + 16, lane : lane + 512] = rows[
                first : first + 16, col : col + 512
            ]


def down_chunks(rows, width, wide):
    packed = rows * width // wide
    places = [(row, col) for col in range(0, width, 512) for row in range(0, rows, 16)]
    return [(place, (16 * i % packed, 16 * i // packed * 512)) for i, place in enumerate(places)]


def pack_kernel(down_ref, out_ref):
    rows, width = out_ref.shape[0] * out_ref.shape[1] // down_ref.shape[1], down_ref.shape[1]
    held = down_ref[...]
    held = jnp.concatenate([held, jnp.zeros((rows - held.shape[0], width), low)], axis=0)
    for (row, col), (to, lane) in down_chunks(rows, width, out_ref.shape[1]):
        out_ref[to : to + 16, lane : lane + 512] = held[row : row + 16, col : col + 512]


def pack(down, rows, wide):
    return pl.pallas_call(
        pack_kernel,
        out_shape=jax.ShapeDtypeStruct((rows * down.shape[1] // wide, wide), low),
        compiler_params=pltpu.CompilerParams(vmem_limit_bytes=8 << 20),
        cost_estimate=FILLS,
    )(down)


def unpack_down(packed, rows, width):
    parts = {
        place: packed[to : to + 16, lane : lane + 512]
        for place, (to, lane) in down_chunks(rows, width, packed.shape[1])
    }
    return jnp.concatenate(
        [jnp.concatenate([parts[row, col] for col in range(0, width, 512)], axis=1) for row in range(0, rows, 16)],
        axis=0,
    )


def feed_terms(rows, dy_rows, activated, grad_gate, grad_up):
    half, width = rows[0].shape
    units = activated[0].shape[1]
    block = width // N_FLEET
    tall = block // 2 + units // N_FLEET // 2 * width // (2 * units)
    whole = lambda wide: pl.BlockSpec((half, wide), lambda s: (0, 0))
    cut = pl.BlockSpec((half, block), lambda s: (0, s))
    return pl.pallas_call(
        terms_kernel,
        grid=(N_FLEET,),
        in_specs=[cut] * 2 + [whole(width)] * 2 + [whole(units)] * 6,
        out_specs=pl.BlockSpec((2, 1, tall, 2 * units), lambda s: (0, s, 0, 0)),
        out_shape=pltpu.HBM((2, N_FLEET, tall, 2 * units), low),
        scratch_shapes=[pltpu.VMEM((units, width), low)],
        compiler_params=pltpu.CompilerParams(vmem_limit_bytes=28 << 20),
        cost_estimate=pl.CostEstimate(flops=10**10, bytes_accessed=2 * 10**7, transcendentals=0),
    )(*rows, *dy_rows, *activated, *grad_gate, *grad_up)


def down_kernel(left0_ref, left1_ref, right_ref, here_ref, there_ref):
    here_ref[...] = matmul(left0_ref[...], right_ref[...])
    there_ref[...] = matmul(left1_ref[...], right_ref[...]).astype(low)


def down_parts(left, right):
    half, depth = left[0].shape
    width = right.shape[1]
    whole = pl.BlockSpec((half, depth), lambda j: (0, 0))
    tile = pl.BlockSpec((half, 512), lambda j: (0, j))
    return pl.pallas_call(
        down_kernel,
        grid=(width // 512,),
        in_specs=[whole, whole, pl.BlockSpec((depth, 512), lambda j: (0, j))],
        out_specs=[tile, tile],
        out_shape=[jax.ShapeDtypeStruct((half, width), full), jax.ShapeDtypeStruct((half, width), low)],
        compiler_params=pltpu.CompilerParams(vmem_limit_bytes=16 << 20),
        cost_estimate=FILLS,
    )(*left, right)


def segment_numbers(positions, lengths):
    row_ends = jnp.cumsum(lengths)
    return jnp.sum((positions[..., None] >= row_ends).astype(jnp.int32), axis=-1)


def probabilities(query, keys, mask):
    scores = matmul_right_t(query, keys) * SCALE
    scores = jnp.where(mask > 0, scores, -1e30)
    weights = jnp.exp(scores - jnp.max(scores, axis=-1, keepdims=True))
    return weights / jnp.sum(weights, axis=-1, keepdims=True)


def attend_kernel(place, q_ref, k_ref, v_ref, kp_ref, vp_ref, halo_ref, mask_ref, out_ref):
    mask = mask_ref[0]
    wide = q_ref.shape[1]
    at_start = pl.program_id(0) == 0
    for head in range(wide // HEAD):
        at = slice(head * HEAD, (head + 1) * HEAD)
        at_value = slice(wide + head * HEAD, wide + (head + 1) * HEAD)
        keys = jnp.concatenate([jnp.where(at_start, halo_ref[:, at], kp_ref[:, at]), k_ref[:, at]], axis=0)
        values = jnp.concatenate([jnp.where(at_start, halo_ref[:, at_value], vp_ref[:, at]), v_ref[:, at]], axis=0)
        probs = probabilities(q_ref[:, at], keys, mask)
        out_ref[:, at] = matmul(probs.astype(low), values).astype(low)


def block_gradients(query, keys, values, mask, grad_mixed):
    probs = probabilities(query, keys, mask)
    grad_probs = matmul_right_t(grad_mixed, values)
    inner = jnp.sum(probs * grad_probs, axis=-1, keepdims=True)
    return (probs * (grad_probs - inner)).astype(low), probs.astype(low)


def halo_back_kernel(place, q_ref, k_ref, v_ref, halo_ref, mask_ref, gm_ref, back_ref):
    wide = q_ref.shape[1]
    for head in range(wide // HEAD):
        at = slice(head * HEAD, (head + 1) * HEAD)
        at_value = slice(wide + head * HEAD, wide + (head + 1) * HEAD)
        keys = jnp.concatenate([halo_ref[:, at], k_ref[:, at]], axis=0)
        values = jnp.concatenate([halo_ref[:, at_value], v_ref[:, at]], axis=0)
        grad_scores, probs = block_gradients(q_ref[:, at], keys, values, mask_ref[0], gm_ref[:, at])
        back_ref[:, at] = (matmul_left_t(grad_scores, q_ref[:, at])[:WIN] * SCALE).astype(low)
        back_ref[:, at_value] = matmul_left_t(probs, gm_ref[:, at])[:WIN].astype(low)


def halo_back(place, qkv, halo, mask, grad_mixed):
    wide = qkv.shape[1] // 3
    block = lambda column: pl.BlockSpec((BLOCK, wide), lambda s, place: (place[0], column))
    once = pl.BlockSpec((WIN, 2 * wide), lambda s, place: (0, 0))
    return pl.pallas_call(
        halo_back_kernel,
        grid_spec=pltpu.PrefetchScalarGridSpec(
            num_scalar_prefetch=1,
            grid=(1,),
            in_specs=[block(0), block(1), block(2), once]
            + [pl.BlockSpec((1, BLOCK, BLOCK + WIN), lambda s, place: (place[0], 0, 0)), block(0)],
            out_specs=once,
        ),
        out_shape=jax.ShapeDtypeStruct((WIN, 2 * wide), low),
        compiler_params=pltpu.CompilerParams(vmem_limit_bytes=8 << 20),
        cost_estimate=FILLS,
    )(place, qkv, qkv, qkv, halo, mask, grad_mixed)


def attend_back_kernel(
    place, q_ref, k_ref, v_ref, kp_ref, vp_ref, halo_ref, mask_ref, gm_ref, grads_ref, tail_ref, carry
):
    step = pl.program_id(0)
    mask = mask_ref[0]
    wide = q_ref.shape[1]
    at_start = step == N_TEAM - 1

    @pl.when(step == 0)
    def _():
        carry[...] = jnp.zeros_like(carry)

    for head in range(wide // HEAD):
        at = slice(head * HEAD, (head + 1) * HEAD)
        at_value = slice(wide + head * HEAD, wide + (head + 1) * HEAD)
        query = q_ref[:, at]
        keys = jnp.concatenate([jnp.where(at_start, halo_ref[:, at], kp_ref[:, at]), k_ref[:, at]], axis=0)
        values = jnp.concatenate([jnp.where(at_start, halo_ref[:, at_value], vp_ref[:, at]), v_ref[:, at]], axis=0)
        grad_mixed = gm_ref[:, at]
        grad_scores, probs = block_gradients(query, keys, values, mask, grad_mixed)
        grads_ref[:, at] = (matmul(grad_scores, keys) * SCALE).astype(low)
        grad_keys = matmul_left_t(grad_scores, query) * SCALE
        grad_values = matmul_left_t(probs, grad_mixed)
        for here, grad in ((at, grad_keys), (at_value, grad_values)):
            there = slice(wide + here.start, wide + here.stop)
            last = grad[BLOCK:] + carry[:, here]
            grads_ref[: BLOCK - WIN, there] = grad[WIN:BLOCK].astype(low)
            grads_ref[BLOCK - WIN :, there] = last.astype(low)

            @pl.when(step == 0)
            def _(last=last, here=here):
                tail_ref[:, here] = last

            carry[:, here] = grad[:WIN]


def attention_specs(wide, step):
    def block(rows, column, first):
        return pl.BlockSpec((rows, wide), lambda s, place: (place[first + step(s)], column))

    return [
        block(BLOCK, 0, 0),
        block(BLOCK, 1, 0),
        block(BLOCK, 2, 0),
        block(WIN, 1, N_TEAM),
        block(WIN, 2, N_TEAM),
        pl.BlockSpec((WIN, 2 * wide), lambda s, place: (0, 0)),
        pl.BlockSpec((1, BLOCK, BLOCK + WIN), lambda s, place: (place[step(s)], 0, 0)),
    ]


def attend(place, qkv, halo, mask):
    wide = qkv.shape[1] // 3
    return pl.pallas_call(
        attend_kernel,
        grid_spec=pltpu.PrefetchScalarGridSpec(
            num_scalar_prefetch=1,
            grid=(N_TEAM,),
            in_specs=attention_specs(wide, lambda s: s),
            out_specs=pl.BlockSpec((BLOCK, wide), lambda s, place: (place[s], 0)),
        ),
        out_shape=jax.ShapeDtypeStruct((N_TEAM * BLOCK, wide), low),
        compiler_params=pltpu.CompilerParams(vmem_limit_bytes=8 << 20),
        cost_estimate=FILLS,
    )(place, qkv, qkv, qkv, qkv, qkv, halo, mask)


def attend_back(place, qkv, halo, mask, grad_mixed):
    wide = qkv.shape[1] // 3
    step = lambda s: N_TEAM - 1 - s
    by_block = lambda width: pl.BlockSpec((BLOCK, width), lambda s, place: (place[step(s)], 0))
    once = pl.BlockSpec((WIN, 2 * wide), lambda s, place: (0, 0))
    return pl.pallas_call(
        attend_back_kernel,
        grid_spec=pltpu.PrefetchScalarGridSpec(
            num_scalar_prefetch=1,
            grid=(N_TEAM,),
            in_specs=attention_specs(wide, step) + [by_block(wide)],
            out_specs=[by_block(3 * wide), once],
            scratch_shapes=[pltpu.VMEM((WIN, 2 * wide), full)],
        ),
        out_shape=[
            jax.ShapeDtypeStruct((N_TEAM * BLOCK, 3 * wide), low),
            jax.ShapeDtypeStruct((WIN, 2 * wide), full),
        ],
        compiler_params=pltpu.CompilerParams(vmem_limit_bytes=8 << 20),
        cost_estimate=FILLS,
    )(place, qkv, qkv, qkv, qkv, qkv, halo, mask, grad_mixed)


def attn_terms_kernel(normed_ref, grad_ref, mixed_ref, hidden0_ref, hidden1_ref, out_ref, out_term):
    step = pl.program_id(0)
    half = hidden0_ref.shape[0]
    wide, deep = mixed_ref.shape[1], grad_ref.shape[1]
    rows = wide // N_FLEET

    @pl.when(step == 0)
    def _():
        out_term[...] = (
            matmul_left_t(mixed_ref[:half], hidden0_ref[...]) + matmul_left_t(mixed_ref[half:], hidden1_ref[...])
        ).astype(low)

    out_ref[:, :deep] = matmul_left_t(normed_ref[...], grad_ref[...]).astype(low)
    part = out_term[pl.ds(pl.multiple_of(step * rows, 32), rows)]
    for t in range(N_TEAM):
        out_ref[rows * t : rows * (t + 1), deep:] = part[:, wide * t : wide * (t + 1)]


def attn_terms(normed, grad_qkv, mixed, hidden_low):
    rows, width = normed.shape
    half, wide, deep = rows // 2, mixed.shape[1], grad_qkv.shape[1]
    block = width // N_FLEET
    whole = lambda shape: pl.BlockSpec(shape, lambda s: (0, 0))
    return pl.pallas_call(
        attn_terms_kernel,
        grid=(N_FLEET,),
        in_specs=[pl.BlockSpec((rows, block), lambda s: (0, s)), whole((rows, deep)), whole((rows, wide))]
        + [whole((half, width))] * 2,
        out_specs=pl.BlockSpec((block, deep + wide), lambda s: (s, 0)),
        out_shape=pltpu.HBM((width, deep + wide), low),
        scratch_shapes=[pltpu.VMEM((wide, width), low)],
        compiler_params=pltpu.CompilerParams(vmem_limit_bytes=18 << 20),
        cost_estimate=FILLS,
    )(normed, grad_qkv, mixed, *hidden_low)


def summed(refs, at):
    return refs[0][at] + sum(ref[at].astype(full) for ref in refs[1:])


def own_rows(kernel, out_types, *operands):
    shape = operands[0].shape
    n = len(operands)

    def whole(*refs):
        sources, outs, held, arrived = refs[:n], refs[n:-n - 1], refs[-n - 1 : -1], refs[-1]
        copies = [pltpu.make_async_copy(sources[i], held[i], arrived.at[i]) for i in range(n)]
        for copy in copies:
            copy.start()
        for copy in copies:
            copy.wait()
        for first in range(0, shape[0], 16):
            kernel(slice(first, first + 16), (*held, *outs))

    return pl.pallas_call(
        whole,
        in_specs=[pl.BlockSpec(memory_space=pl.ANY)] * n,
        out_shape=[jax.ShapeDtypeStruct(shape, dtype) for dtype in out_types],
        scratch_shapes=[pltpu.VMEM(operand.shape, operand.dtype) for operand in operands]
        + [pltpu.SemaphoreType.DMA((n,))],
        compiler_params=pltpu.CompilerParams(vmem_limit_bytes=12 << 20),
        cost_estimate=FILLS,
    )(*operands)


def hidden_kernel(at, refs):
    *parts, x_ref, gain_ref, hidden_ref, again_ref = refs
    hidden = x_ref[at].astype(full) + summed(parts, at)
    hidden_ref[at] = hidden
    again_ref[at] = (hidden * inverse_rms(hidden) * gain_ref[...]).astype(low)


def norm_backward(grad_normed, inputs, gain):
    scale_rows = inverse_rms(inputs)
    weighted = grad_normed * gain
    return scale_rows * weighted - inputs * scale_rows**3 * jnp.mean(
        weighted * inputs, axis=-1, keepdims=True
    )


def grad_hidden_kernel(at, refs):
    *parts, hidden_ref, dy_ref, gain_ref, grad_ref, low_ref = refs
    grad = dy_ref[at].astype(full) + norm_backward(summed(parts, at), hidden_ref[at], gain_ref[...])
    grad_ref[at] = grad
    low_ref[at] = grad.astype(low)


def input_grad_kernel(at, refs):
    *parts, x_ref, grad_ref, gain_ref, out_ref = refs
    out_ref[at] = grad_ref[at] + norm_backward(summed(parts, at), x_ref[at].astype(full), gain_ref[...])


def outputs_kernel(at, refs):
    *parts, hidden_ref, out_ref = refs
    out_ref[at] = (hidden_ref[at] + summed(parts, at)).astype(low)


def feed_owner_kernel(unit_rows, group, here_ref, there_ref, w_gate_ref, w_up_ref, gain_ref, gate_ref, up_ref, grad_ref):
    rows = here_ref.shape[1]
    units = here_ref.shape[2] // 2
    pad = units // N_FLEET
    first = group[0] == 0
    for t in range(N_TEAM):
        here, there = here_ref[t], there_ref[t]
        block = jnp.concatenate([jnp.where(first, here, there), jnp.where(first, there, here)], axis=0).astype(full)
        for i, out_ref in enumerate((gate_ref, up_ref)):
            for f in range(N_FLEET):
                at = i * units + f * pad
                to = (f * N_TEAM + t) * unit_rows
                out_ref[:, to : to + unit_rows] = block[:, at : at + unit_rows]
    for row in range(0, 2 * rows, 16):
        at = slice(row, row + 16)
        total = w_gate_ref[at].astype(full) * gate_ref[at] + w_up_ref[at].astype(full) * up_ref[at]
        grad_ref[at] = jnp.sum(total, axis=1, keepdims=True) / gain_ref[at].astype(full)


def feed_owner(group, here, there, w_gate, w_up, gain):
    shard, wide = w_gate.shape
    vmem = pl.BlockSpec(memory_space=pltpu.VMEM)
    return pl.pallas_call(
        functools.partial(feed_owner_kernel, wide // (N_FLEET * N_TEAM)),
        in_specs=[pl.BlockSpec(memory_space=pltpu.SMEM)] + [vmem] * 5,
        out_specs=[vmem] * 3,
        out_shape=[jax.ShapeDtypeStruct((shard, wide), full)] * 2 + [jax.ShapeDtypeStruct((shard, 1), full)],
        compiler_params=pltpu.CompilerParams(vmem_limit_bytes=10 << 20),
        cost_estimate=FILLS,
    )(group, here, there, w_gate, w_up, gain[:, None])


def attn_owner_kernel(
    sums_ref, out0_ref, out1_ref, w_query_ref, w_key_ref, w_value_ref, gain_ref,
    query_ref, key_ref, value_ref, out_ref, grad_ref,
):
    wide = sums_ref.shape[2] // 3
    weights = (w_query_ref, w_key_ref, w_value_ref)
    total = jnp.zeros((query_ref.shape[0], wide), full)
    for t in range(N_TEAM):
        to = slice(t * wide, (t + 1) * wide)
        block = sums_ref[t].astype(full) + sums_ref[N_TEAM + t].astype(full)
        for i, grad in enumerate((query_ref, key_ref, value_ref)):
            part = block[:, i * wide : (i + 1) * wide]
            grad[:, to] = part
            total += part * weights[i][:, to].astype(full)
        out_ref[:, to] = out0_ref[t].astype(full) + out1_ref[t].astype(full)
    grad_ref[...] = jnp.sum(total, axis=1, keepdims=True) / gain_ref[...].astype(full)


def attn_owner(sums, out_sums, w_query, w_key, w_value, gain):
    grad = jax.ShapeDtypeStruct(w_query.shape, full)
    return pl.pallas_call(
        attn_owner_kernel,
        out_shape=[grad] * 4 + [jax.ShapeDtypeStruct((w_query.shape[0], 1), full)],
        compiler_params=pltpu.CompilerParams(vmem_limit_bytes=8 << 20),
        cost_estimate=FILLS,
    )(sums, *out_sums, w_query, w_key, w_value, gain[:, None])


def body(
    tokens, lengths, norm_gain, w_query, w_key, w_value, w_out, mlp_gain, w_gate, w_up, w_down, cotangent
):
    rows, width = tokens.shape
    shard = w_query.shape[0]
    team_wide = width // N_TEAM
    unit_rows = w_down.shape[0]
    unit_pad = -(-unit_rows // 32) * 32
    units = N_FLEET * unit_pad
    x, yl, z, c = [lax.axis_index(axis) for axis in ("x", "yl", "z", "c")]
    fleet = lax.axis_index(FLEET)

    order = jnp.arange(N_TEAM, dtype=jnp.int32)
    spot = (jnp.bitwise_xor(order % N_C, c) * N_Z + (order // N_C - z) % N_Z).astype(jnp.int32)
    before = jnp.concatenate([jnp.zeros((1,), jnp.int32), 2 * spot[:-1] + 1])
    place = jnp.concatenate([spot, before])
    last_spot = (1 - c) * N_Z + N_Z - 1 - z
    last_at = last_spot * BLOCK + BLOCK - WIN
    kept = jnp.arange(N_TEAM, dtype=jnp.int32)
    kept_block = N_C * ((kept % N_Z + z) % N_Z) + jnp.bitwise_xor(kept // N_Z, c)
    first_pos = (fleet * N_TEAM + kept_block) * BLOCK
    query_pos = first_pos[:, None] + jnp.arange(BLOCK, dtype=jnp.int32)
    key_pos = first_pos[:, None] - WIN + jnp.arange(BLOCK + WIN, dtype=jnp.int32)
    query_segs = segment_numbers(query_pos, lengths[0])
    key_segs = jnp.where(key_pos >= 0, segment_numbers(key_pos, lengths[0]), -1)
    distance = query_pos[:, :, None] - key_pos[:, None, :]
    mask = (distance >= 0) & (distance < WIN) & (query_segs[:, :, None] == key_segs[:, None, :])
    mask = mask.astype(full)

    out_there = swapped(w_out)
    x_mine = [tokens, from_ahead(tokens, "z", 1), None, from_ahead(tokens, "z", 3)]
    cut = attn_cut(w_query, w_key, w_value, norm_gain, mlp_gain)
    cut = lax.all_to_all(cut, TEAM, 0, 0, tiled=True).reshape(N_TEAM * shard, -1)
    out_cut = out_there.reshape(shard, N_TEAM, team_wide).transpose(1, 0, 2)
    out_cut = out_cut.reshape(N_TEAM * shard, team_wide)
    cut, out_cut, x_mine, w_gate_later, dy = lax.optimization_barrier((cut, out_cut, x_mine, w_gate, cotangent))
    qkv_piece, rest = cut[:, : 3 * team_wide], jnp.concatenate([cut[:, 3 * team_wide :], out_cut], axis=1)
    along_y = lambda value, by: from_ahead(value, ("g", "yl"), by)
    other = lambda block: from_ahead(block, "c", 1)
    attn = lax.all_to_all(jnp.broadcast_to(qkv_piece, (N_X, *qkv_piece.shape)), "x", 0, 0, tiled=True)
    attn = attn.reshape(width // 2, -1)
    half_rest = rest.shape[0] // 2
    rest_there = along_y(rest[:half_rest], 1), along_y(rest[half_rest:], -1)
    x_mine[2] = from_ahead(x_mine[0], "z", 2)
    x_other = [other(x_mine[0]), other(x_mine[1]), None, other(x_mine[3])]
    gate_up = feed_cut(w_gate_later, w_up, unit_rows, units)
    down_piece = pack(w_down, unit_pad, 2 * units)
    attn, rest_there, x_mine, x_other, dy, gate_up, down_piece, place, mask = lax.optimization_barrier(
        (attn, rest_there, x_mine, x_other, dy, gate_up, down_piece, place, mask)
    )
    pair = jnp.concatenate([rest, *rest_there], axis=0)
    pairs = [pair] + [from_ahead(pair, "x", k) for k in (1, 2, 3)]
    x_other[2] = other(x_mine[2])
    gate_up_piece = lax.all_to_all(gate_up, TEAM, 0, 0, tiled=True).reshape(N_TEAM * shard, -1)
    attn_there = along_y(attn[: width // 4], 1), along_y(attn[width // 4 :], -1)
    attn, attn_there, pairs, x_mine, x_other, dy, gate_up_piece = lax.optimization_barrier(
        (attn, attn_there, pairs, x_mine, x_other, dy, gate_up_piece)
    )
    dy_mine = [dy, from_ahead(dy, "z", 1), None, from_ahead(dy, "z", 3)]
    x_blocks = x_mine + x_other
    halo = along_line(lax.select_n(last_spot, *[block[BLOCK - WIN :] for block in x_blocks]), 1)
    feed_piece = jnp.concatenate([gate_up_piece, down_piece], axis=0)
    w_feed = lax.all_gather(feed_piece, FLEET, axis=0, tiled=False)

    half = N_Z * BLOCK
    w_qkv, w_out_team, gain_rows = assemble(jnp.stack([yl, x]).astype(jnp.int32), attn, attn_there, pairs)
    normed = normalised(x_blocks, gain_rows)
    gain_one, gain_two = gain_rows[:1], gain_rows[1:2]
    qkv = matmul(normed, w_qkv).astype(low)
    qkv, dy_mine, halo = lax.optimization_barrier((qkv, dy_mine, halo))
    dy_mine[2] = from_ahead(dy_mine[0], "z", 2)
    halo = halo.astype(full)
    halo = matmul((halo * inverse_rms(halo) * gain_one).astype(low), w_qkv[:, team_wide:]).astype(low)
    mixed = attend(place, qkv, halo, mask)
    halves = lambda rows: (rows[:half], rows[half : 2 * half])
    hidden_blocks = core_sum(halves(mixed), lambda rows: matmul(rows, w_out_team))
    hidden_blocks, dy_mine = lax.optimization_barrier((hidden_blocks, dy_mine))
    dy_other = [other(block) for block in dy_mine]
    hidden_parts, dy_mine, dy_other = lax.optimization_barrier((z_send(hidden_blocks), dy_mine, dy_other))

    hidden, again = own_rows(hidden_kernel, (full, low), *hidden_parts, tokens, gain_two)
    again = z_gather(again)
    again_other = [other(block) for block in again[:2]] + [None, other(again[3])]
    again, again_other[:2], again_other[3] = lax.optimization_barrier((again, again_other[:2], again_other[3]))
    again_other[2] = other(again[2])
    w_gate_up, w_down_team = unpack(w_feed, N_TEAM * shard, unit_pad, width)
    act_mine, gate_mine, up_mine, x_mine, dy_mine = feed(again, dy_mine, w_gate_up, w_down_team)
    act_other, gate_other, up_other, x_other, dy_other = feed(again_other, dy_other, w_gate_up, w_down_team)
    there = feed_back(gate_other, up_other, w_gate_up, low)
    again_blocks = core_blocks(feed_back(gate_mine, up_mine, w_gate_up, full), there)
    activated, grad_gate, grad_up = (act_mine, act_other), (gate_mine, gate_other), (up_mine, up_other)
    again_blocks, activated, grad_gate, grad_up = lax.optimization_barrier(
        (again_blocks, activated, grad_gate, grad_up)
    )
    mlp_term = feed_terms((x_mine, x_other), (dy_mine, dy_other), activated, grad_gate, grad_up)
    again_parts = z_send(again_blocks)
    mlp_term, again_parts[1], again_parts[3] = lax.optimization_barrier((mlp_term, again_parts[1], again_parts[3]))
    mlp_sum = lax.psum_scatter(
        mlp_term.reshape(-1, 2 * units), ("g", *FLEET), scatter_dimension=0, tiled=True
    )

    grad_hidden, hidden_low = own_rows(grad_hidden_kernel, (full, low), *again_parts, hidden, cotangent, gain_two)
    output_parts = down_parts(activated, w_down_team)
    hidden_low, output_parts = lax.optimization_barrier((z_gather(hidden_low), output_parts))
    hidden_low = [join(hidden_low)]
    hidden_low.append(other(hidden_low[0]))
    output_blocks = core_blocks(*output_parts)

    grad_mixed = [matmul_right_t(rows, w_out_team).astype(low) for rows in hidden_low]
    grad_mixed = jnp.concatenate(grad_mixed, axis=0)
    back = halo_back(place, qkv, halo, mask, grad_mixed)
    grad_qkv, tail = attend_back(place, qkv, halo, mask, grad_mixed)
    tail = tail + along_line(back, -1).astype(full)
    grad_qkv = lax.dynamic_update_slice(grad_qkv, tail.astype(low), (last_at, team_wide))
    attn_term = attn_terms(normed, grad_qkv, mixed, hidden_low)
    attn_term, grad_qkv, output_parts = lax.optimization_barrier((attn_term, grad_qkv, z_send(output_blocks)))
    attn_sum = lax.psum_scatter(attn_term, FLEET, scatter_dimension=0, tiled=True)
    (outputs,) = own_rows(outputs_kernel, (low,), *output_parts, hidden)
    normed_blocks = core_sum(halves(grad_qkv), lambda rows: matmul_right_t(rows, w_qkv))

    down_sum = unpack_down(mlp_sum[N_TEAM * shard // 2 :], unit_pad // 2, width)
    gate_up_sum = mlp_sum[: N_TEAM * shard // 2].reshape(N_TEAM, shard // 2, 2 * units)
    gate_up_sum = lax.all_to_all(gate_up_sum, TEAM, 0, 0, tiled=True)
    normed_blocks, gate_up_sum, down_sum = lax.optimization_barrier((normed_blocks, gate_up_sum, down_sum))
    gate_up_there, down_there = from_ahead(gate_up_sum, "g", 1), from_ahead(down_sum, "g", 1)
    normed_parts, attn_sum, outputs, gate_up_there, down_there = lax.optimization_barrier(
        (z_send(normed_blocks), attn_sum, outputs, gate_up_there, down_there)
    )
    (input_grad,) = own_rows(input_grad_kernel, (full,), *normed_parts, tokens, grad_hidden, gain_one)
    qkv_sum = attn_sum[:, : 3 * team_wide].reshape(N_TEAM, shard, 3 * team_wide)
    qkv_sum = lax.all_to_all(jnp.concatenate([qkv_sum, qkv_sum], axis=0), ("g", *TEAM), 0, 0, tiled=True)
    out_sum = attn_sum[:, 3 * team_wide :].reshape(N_TEAM, shard, team_wide)
    group = lax.axis_index("g")
    gate_grad, up_grad, mlp_gain_grad = feed_owner(
        group[None].astype(jnp.int32), gate_up_sum, gate_up_there, w_gate, w_up, mlp_gain
    )
    qkv_sum, out_sums, input_grad, gate_grad = lax.optimization_barrier(
        (qkv_sum, (swapped(out_sum), swapped(out_sum, 1)), input_grad, gate_grad)
    )
    query_grad, key_grad, value_grad, out_grad, gain_grad = attn_owner(
        qkv_sum, out_sums, w_query, w_key, w_value, norm_gain
    )
    first, second = jnp.where(group == 0, down_sum, down_there), jnp.where(group == 0, down_there, down_sum)
    down_grad = jnp.concatenate([first, second], axis=0)[:unit_rows].astype(full)
    return (
        outputs,
        input_grad,
        gain_grad[:, 0],
        query_grad,
        key_grad,
        value_grad,
        out_grad,
        mlp_gain_grad[:, 0],
        gate_grad,
        up_grad,
        down_grad,
    )


def solution(mesh):
    fine = Mesh(mesh.devices.reshape(2, 2, 4, 4, 2), ALL)
    return jax.shard_map(
        body,
        mesh=fine,
        in_specs=(
            P(ALL, None),
            P("g", None),
            P(SEQ),
            P(SEQ, None),
            P(SEQ, None),
            P(SEQ, None),
            P(SEQ, None),
            P(SEQ),
            P(SEQ, None),
            P(SEQ, None),
            P(SEQ, None),
            P(ALL, None),
        ),
        out_specs=(
            P(ALL, None),
            P(ALL, None),
            P(SEQ),
            P(SEQ, None),
            P(SEQ, None),
            P(SEQ, None),
            P(SEQ, None),
            P(SEQ),
            P(SEQ, None),
            P(SEQ, None),
            P(SEQ, None),
        ),
        check_vma=False,
    )
```

```python
import functools

import jax
import jax.numpy as jnp
from jax import lax
from jax.experimental import pallas as pl
from jax.experimental.pallas import tpu as pltpu
from jax.sharding import Mesh
from jax.sharding import PartitionSpec as P

FILLS = pl.CostEstimate(flops=1, bytes_accessed=1, transcendentals=0)
HEAD = 128
WIN = 64
BLOCK = 128
epsilon = 1e-06

TEAM = ("z", "c")
FLEET = ("yl", "x")
SEQ = ("yl", "x", "z", "c")
ALL = ("g", "yl", "x", "z", "c")
N_X, N_Z, N_C, N_TEAM, N_FLEET = 4, 4, 2, 8, 8
SCALE = HEAD ** (-0.5)
low = jnp.bfloat16
full = jnp.float32


def from_ahead(value, axis, by):
    n = lax.axis_size(axis)
    return lax.ppermute(value, axis, [((i + by) % n, i) for i in range(n)])


def along_line(value, by):
    return lax.ppermute(
        value, FLEET, [(i, i + by) for i in range(N_FLEET) if 0 <= i + by < N_FLEET]
    )


def swapped(value, across=0):
    n = N_FLEET * N_TEAM
    pairs = [(N_TEAM * f + t, N_TEAM * t + f) for f in range(N_FLEET) for t in range(N_TEAM)]
    return lax.ppermute(value, ALL, [(g * n + a, (g ^ across) * n + b) for g in range(2) for a, b in pairs])


def z_gather(value):
    return [value] + [from_ahead(value, "z", k) for k in (1, 2, 3)]


def z_send(blocks):
    return [blocks[0]] + [from_ahead(blocks[k], "z", -k) for k in (1, 2, 3)]


def core_sum(left, right):
    there = right(left[1]).astype(low)
    return core_blocks(right(left[0]), there)


def inverse_rms(values):
    return lax.rsqrt(jnp.mean(values * values, axis=-1, keepdims=True) + epsilon)


def matmul(left, right):
    return jnp.dot(left, right, preferred_element_type=full)


def matmul_left_t(left, right):
    return lax.dot_general(left, right, (((0,), (0,)), ((), ())), preferred_element_type=full)


def matmul_right_t(left, right):
    return lax.dot_general(left, right, (((1,), (1,)), ((), ())), preferred_element_type=full)


def attn_cut_kernel(gain_ref, mlp_gain_ref, *refs):
    sources, out_ref, held, rows, arrived = refs[:3], refs[3], refs[4:7], refs[7], refs[8]
    copies = [pltpu.make_async_copy(sources[i], held[i], arrived.at[i]) for i in range(3)]
    for copy in copies:
        copy.start()
    shard, width = sources[0].shape
    wide = width // N_TEAM
    rows[...] = jnp.zeros_like(rows)
    rows[0:1, :shard] = gain_ref[...].astype(full)
    rows[1:2, :shard] = mlp_gain_ref[...].astype(full)
    gains = rows[...].T[:shard].astype(low)
    out_ref[:, :, 3 * wide :] = jnp.zeros((N_TEAM, shard, out_ref.shape[2] - 3 * wide), low)
    for copy in copies:
        copy.wait()
    for t in range(N_TEAM):
        for i, ref in enumerate(held):
            out_ref[t, :, i * wide : (i + 1) * wide] = ref[:, t * wide : (t + 1) * wide]
        out_ref[t, :, 3 * wide : 3 * wide + 8] = gains


def attn_cut(w_query, w_key, w_value, norm_gain, mlp_gain):
    shard, width = w_query.shape
    vmem = pl.BlockSpec(memory_space=pltpu.VMEM)
    return pl.pallas_call(
        attn_cut_kernel,
        in_specs=[vmem] * 2 + [pl.BlockSpec(memory_space=pl.ANY)] * 3,
        out_shape=jax.ShapeDtypeStruct((N_TEAM, shard, 3 * width // N_TEAM + 128), low),
        scratch_shapes=[pltpu.VMEM((shard, width), low)] * 3
        + [pltpu.VMEM((8, 128), full), pltpu.SemaphoreType.DMA((3,))],
        compiler_params=pltpu.CompilerParams(vmem_limit_bytes=8 << 20),
    )(norm_gain[None], mlp_gain[None], w_query, w_key, w_value)


def assemble_kernel(at, own_ref, low_ref, high_ref, *refs):
    *pair_refs, qkv_ref, out_ref, gain_ref = refs
    yl, x = at[0], at[1]
    rows = own_ref.shape[0]
    qkv_ref[pl.ds(pl.multiple_of(yl * rows, 256), rows)] = own_ref[...]
    there = (1 - yl) * rows
    qkv_ref[pl.ds(pl.multiple_of(there, 256), rows // 2)] = low_ref[...]
    qkv_ref[pl.ds(pl.multiple_of(there + rows // 2, 256), rows // 2)] = high_ref[...]
    block, wide = pair_refs[0].shape[0] // 2, pair_refs[0].shape[1] - 128
    shard = block // N_TEAM
    for k, pair_ref in enumerate(pair_refs):
        for side in range(2):
            fleet = (yl + side) % 2 * N_X + (x + k) % N_X
            piece = slice(side * block, (side + 1) * block)
            gains = pair_ref[piece, :128].astype(full).T[: gain_ref.shape[0]]
            gain_ref[:, pl.ds(pl.multiple_of(fleet * block, 256), block)] = gains
            to = pl.ds(pl.multiple_of(fleet * shard, 32), shard)
            for t in range(N_TEAM):
                first = side * block + t * shard
                out_ref[to, t * wide : (t + 1) * wide] = pair_ref[first : first + shard, 128:]


def assemble(at, own, there, pairs):
    width, wide = 2 * own.shape[0], pairs[0].shape[1] - 128
    vmem = pl.BlockSpec(memory_space=pltpu.VMEM)
    return pl.pallas_call(
        assemble_kernel,
        in_specs=[pl.BlockSpec(memory_space=pltpu.SMEM)] + [vmem] * (3 + N_X),
        out_specs=[vmem] * 3,
        out_shape=[
            jax.ShapeDtypeStruct((width, own.shape[1]), low),
            jax.ShapeDtypeStruct((wide, width), low),
            jax.ShapeDtypeStruct((8, width), full),
        ],
        compiler_params=pltpu.CompilerParams(vmem_limit_bytes=16 << 20),
        cost_estimate=FILLS,
    )(at, own, *there, *pairs)


def feed_cut_kernel(unit_rows, gate_ref, up_ref, out_ref):
    units = out_ref.shape[2] // 2
    pad = units // N_FLEET
    out_ref[...] = jnp.zeros(out_ref.shape, low)
    for t in range(N_TEAM):
        for i, ref in enumerate((gate_ref, up_ref)):
            for f in range(N_FLEET):
                at = i * units + f * pad
                first = (f * N_TEAM + t) * unit_rows
                out_ref[t, :, at : at + unit_rows] = ref[:, first : first + unit_rows]


def feed_cut(w_gate, w_up, unit_rows, units):
    return pl.pallas_call(
        functools.partial(feed_cut_kernel, unit_rows),
        out_shape=jax.ShapeDtypeStruct((N_TEAM, w_gate.shape[0], 2 * units), low),
        compiler_params=pltpu.CompilerParams(vmem_limit_bytes=8 << 20),
        cost_estimate=FILLS,
    )(w_gate, w_up)


def join_kernel(*refs):
    rows = refs[0].shape[0]
    for i, ref in enumerate(refs[:-1]):
        refs[-1][i * rows : (i + 1) * rows] = ref[...]


def join(blocks):
    rows, width = blocks[0].shape
    return pl.pallas_call(
        join_kernel,
        out_shape=jax.ShapeDtypeStruct((len(blocks) * rows, width), low),
        compiler_params=pltpu.CompilerParams(vmem_limit_bytes=8 << 20),
        cost_estimate=FILLS,
    )(*blocks)


def pair_kernel(here_ref, there_ref, own_ref, *block_refs):
    rows = own_ref.shape[0]
    for i, ref in enumerate((own_ref, *block_refs)):
        at = slice(i * rows, (i + 1) * rows)
        ref[...] = (here_ref[at] + there_ref[at].astype(full)).astype(ref.dtype)


def core_blocks(here, there):
    rows, width = here.shape[0] // N_Z, here.shape[1]
    return pl.pallas_call(
        pair_kernel,
        out_shape=[jax.ShapeDtypeStruct((rows, width), full)] + [jax.ShapeDtypeStruct((rows, width), low)] * 3,
        compiler_params=pltpu.CompilerParams(vmem_limit_bytes=12 << 20),
        cost_estimate=FILLS,
    )(here, from_ahead(there, "c", 1))


def norm_kernel(*refs):
    *block_refs, gain_ref, out_ref = refs
    gain = gain_ref[:1]
    at = 0
    for ref in block_refs:
        for first in range(0, ref.shape[0], 16):
            values = ref[first : first + 16].astype(full)
            out_ref[at + first : at + first + 16] = (values * inverse_rms(values) * gain).astype(low)
        at += ref.shape[0]


def normalised(blocks, gain_rows):
    rows = sum(block.shape[0] for block in blocks)
    return pl.pallas_call(
        norm_kernel,
        out_shape=jax.ShapeDtypeStruct((rows, blocks[0].shape[1]), low),
        compiler_params=pltpu.CompilerParams(vmem_limit_bytes=14 << 20),
        cost_estimate=FILLS,
    )(*blocks, gain_rows)


TILE = 256


def feed_kernel(*refs):
    sources = refs[: 2 * N_Z]
    gate_ref, up_ref, down_ref, act_ref, grad_gate_ref, grad_up_ref, x_ref, dy_ref, arrived = refs[2 * N_Z :]
    rows = sources[0].shape[0]

    @pl.when(pl.program_id(0) == 0)
    def _():
        places = [ref.at[pl.ds(i * rows, rows)] for ref in (x_ref, dy_ref) for i in range(N_Z)]
        copies = [pltpu.make_async_copy(sources[i], places[i], arrived.at[i]) for i in range(2 * N_Z)]
        for copy in copies:
            copy.start()
        for copy in copies:
            copy.wait()

    gate = matmul(x_ref[...], gate_ref[...])
    up = matmul(x_ref[...], up_ref[...])
    grad_act = matmul_right_t(dy_ref[...], down_ref[...])
    sigmoid = jax.nn.sigmoid(gate)
    silu = gate * sigmoid
    act_ref[...] = (silu * up).astype(low)
    grad_gate_ref[...] = (grad_act * up * sigmoid * (1.0 + gate * (1.0 - sigmoid))).astype(low)
    grad_up_ref[...] = (grad_act * silu).astype(low)


def feed(rows, dy_rows, w_gate_up, w_down):
    block, width = rows[0].shape
    units = w_down.shape[0]
    tiles = units // TILE
    whole = pl.BlockSpec((N_Z * block, width), lambda j: (0, 0))
    tile = pl.BlockSpec((N_Z * block, TILE), lambda j: (0, j))
    return pl.pallas_call(
        feed_kernel,
        grid=(tiles,),
        in_specs=[pl.BlockSpec(memory_space=pl.ANY)] * (2 * N_Z)
        + [
            pl.BlockSpec((width, TILE), lambda j: (0, j)),
            pl.BlockSpec((width, TILE), lambda j: (0, tiles + j)),
            pl.BlockSpec((TILE, width), lambda j: (j, 0)),
        ],
        out_specs=[tile] * 3 + [whole] * 2,
        out_shape=[jax.ShapeDtypeStruct((N_Z * block, units), low)] * 3
        + [jax.ShapeDtypeStruct((N_Z * block, width), low)] * 2,
        scratch_shapes=[pltpu.SemaphoreType.DMA((2 * N_Z,))],
        compiler_params=pltpu.CompilerParams(vmem_limit_bytes=24 << 20),
        cost_estimate=FILLS,
    )(*rows, *dy_rows, w_gate_up, w_gate_up, w_down)


def unpack_kernel(packed_ref, gate_up_ref, down_ref):
    block = gate_up_ref.shape[0]
    gate_up_ref[...] = packed_ref[0, :block]
    rows, width = down_ref.shape
    for (row, col), (to, lane) in down_chunks(rows, width, gate_up_ref.shape[1]):
        down_ref[row : row + 16, col : col + 512] = packed_ref[
            0, block + to : block + to + 16, lane : lane + 512
        ]


def unpack(packed, block, rows, width):
    fleet, tall, wide = packed.shape
    return pl.pallas_call(
        unpack_kernel,
        grid=(fleet,),
        in_specs=[pl.BlockSpec((1, tall, wide), lambda s: (s, 0, 0))],
        out_specs=[pl.BlockSpec((block, wide), lambda s: (s, 0)), pl.BlockSpec((rows, width), lambda s: (s, 0))],
        out_shape=[
            jax.ShapeDtypeStruct((fleet * block, wide), low),
            jax.ShapeDtypeStruct((fleet * rows, width), low),
        ],
        compiler_params=pltpu.CompilerParams(vmem_limit_bytes=10 << 20),
        cost_estimate=FILLS,
    )(packed)


def feed_back_kernel(gate_ref, up_ref, right_ref, out_ref):
    units = gate_ref.shape[1]
    out_ref[...] = (
        matmul_right_t(gate_ref[...], right_ref[:, :units]) + matmul_right_t(up_ref[...], right_ref[:, units:])
    ).astype(out_ref.dtype)


def feed_back(grad_gate, grad_up, w_gate_up, dtype):
    rows, units = grad_gate.shape
    width = w_gate_up.shape[0]
    whole = pl.BlockSpec((rows, units), lambda j: (0, 0))
    return pl.pallas_call(
        feed_back_kernel,
        grid=(width // 512,),
        in_specs=[whole, whole, pl.BlockSpec((512, 2 * units), lambda j: (j, 0))],
        out_specs=pl.BlockSpec((rows, 512), lambda j: (0, j)),
        out_shape=jax.ShapeDtypeStruct((rows, width), dtype),
        compiler_params=pltpu.CompilerParams(vmem_limit_bytes=20 << 20),
        cost_estimate=FILLS,
    )(grad_gate, grad_up, w_gate_up)


def terms_kernel(
    x0_ref, x1_ref, dy0_ref, dy1_ref, act0_ref, act1_ref, gate0_ref, gate1_ref, up0_ref, up1_ref, out_ref, down
):
    step = pl.program_id(0)
    units = act0_ref.shape[1]
    pad = units // N_FLEET
    block = x0_ref.shape[1]

    @pl.when(step == 0)
    def _():
        for first in range(0, units, TILE):
            at = slice(first, first + TILE)
            down[at] = (
                matmul_left_t(act0_ref[:, at], dy0_ref[...]) + matmul_left_t(act1_ref[:, at], dy1_ref[...])
            ).astype(low)

    for i, (grad0_ref, grad1_ref) in enumerate(((gate0_ref, gate1_ref), (up0_ref, up1_ref))):
        at = slice(i * units, (i + 1) * units)
        term = matmul_left_t(x0_ref[...], grad0_ref[...]) + matmul_left_t(x1_ref[...], grad1_ref[...])
        term = term.astype(low)
        for row in range(0, block, 32):
            for g in range(2):
                out_ref[g, 0, row // 2 : row // 2 + 16, at] = term[row + 16 * g : row + 16 * g + 16]
    rows = down[pl.ds(pl.multiple_of(step * pad, 16), pad)]
    for g in range(2):
        for (row, col), (to, lane) in down_chunks(pad // 2, rows.shape[1], 2 * units):
            first = g * (pad // 2) + row
            out_ref[g, 0, block // 2 + to : block // 2 + to + 16, lane : lane + 512] = rows[
                first : first + 16, col : col + 512
            ]


def down_chunks(rows, width, wide):
    packed = rows * width // wide
    places = [(row, col) for col in range(0, width, 512) for row in range(0, rows, 16)]
    return [(place, (16 * i % packed, 16 * i // packed * 512)) for i, place in enumerate(places)]


def pack_kernel(down_ref, out_ref):
    rows, width = out_ref.shape[0] * out_ref.shape[1] // down_ref.shape[1], down_ref.shape[1]
    held = down_ref[...]
    held = jnp.concatenate([held, jnp.zeros((rows - held.shape[0], width), low)], axis=0)
    for (row, col), (to, lane) in down_chunks(rows, width, out_ref.shape[1]):
        out_ref[to : to + 16, lane : lane + 512] = held[row : row + 16, col : col + 512]


def pack(down, rows, wide):
    return pl.pallas_call(
        pack_kernel,
        out_shape=jax.ShapeDtypeStruct((rows * down.shape[1] // wide, wide), low),
        compiler_params=pltpu.CompilerParams(vmem_limit_bytes=8 << 20),
        cost_estimate=FILLS,
    )(down)


def unpack_down(packed, rows, width):
    parts = {
        place: packed[to : to + 16, lane : lane + 512]
        for place, (to, lane) in down_chunks(rows, width, packed.shape[1])
    }
    return jnp.concatenate(
        [jnp.concatenate([parts[row, col] for col in range(0, width, 512)], axis=1) for row in range(0, rows, 16)],
        axis=0,
    )


def feed_terms(rows, dy_rows, activated, grad_gate, grad_up):
    half, width = rows[0].shape
    units = activated[0].shape[1]
    block = width // N_FLEET
    tall = block // 2 + units // N_FLEET // 2 * width // (2 * units)
    whole = lambda wide: pl.BlockSpec((half, wide), lambda s: (0, 0))
    cut = pl.BlockSpec((half, block), lambda s: (0, s))
    return pl.pallas_call(
        terms_kernel,
        grid=(N_FLEET,),
        in_specs=[cut] * 2 + [whole(width)] * 2 + [whole(units)] * 6,
        out_specs=pl.BlockSpec((2, 1, tall, 2 * units), lambda s: (0, s, 0, 0)),
        out_shape=pltpu.HBM((2, N_FLEET, tall, 2 * units), low),
        scratch_shapes=[pltpu.VMEM((units, width), low)],
        compiler_params=pltpu.CompilerParams(vmem_limit_bytes=28 << 20),
        cost_estimate=pl.CostEstimate(flops=10**10, bytes_accessed=2 * 10**7, transcendentals=0),
    )(*rows, *dy_rows, *activated, *grad_gate, *grad_up)


def down_kernel(left0_ref, left1_ref, right_ref, here_ref, there_ref):
    here_ref[...] = matmul(left0_ref[...], right_ref[...])
    there_ref[...] = matmul(left1_ref[...], right_ref[...]).astype(low)


def down_parts(left, right):
    half, depth = left[0].shape
    width = right.shape[1]
    whole = pl.BlockSpec((half, depth), lambda j: (0, 0))
    tile = pl.BlockSpec((half, 512), lambda j: (0, j))
    return pl.pallas_call(
        down_kernel,
        grid=(width // 512,),
        in_specs=[whole, whole, pl.BlockSpec((depth, 512), lambda j: (0, j))],
        out_specs=[tile, tile],
        out_shape=[jax.ShapeDtypeStruct((half, width), full), jax.ShapeDtypeStruct((half, width), low)],
        compiler_params=pltpu.CompilerParams(vmem_limit_bytes=16 << 20),
        cost_estimate=FILLS,
    )(*left, right)


def segment_numbers(positions, lengths):
    row_ends = jnp.cumsum(lengths)
    return jnp.sum((positions[..., None] >= row_ends).astype(jnp.int32), axis=-1)


def probabilities(query, keys, mask):
    scores = matmul_right_t(query, keys) * SCALE
    scores = jnp.where(mask > 0, scores, -1e30)
    weights = jnp.exp(scores - jnp.max(scores, axis=-1, keepdims=True))
    return weights / jnp.sum(weights, axis=-1, keepdims=True)


def attend_kernel(place, q_ref, k_ref, v_ref, kp_ref, vp_ref, halo_ref, mask_ref, out_ref):
    mask = mask_ref[0]
    wide = q_ref.shape[1]
    at_start = pl.program_id(0) == 0
    for head in range(wide // HEAD):
        at = slice(head * HEAD, (head + 1) * HEAD)
        at_value = slice(wide + head * HEAD, wide + (head + 1) * HEAD)
        keys = jnp.concatenate([jnp.where(at_start, halo_ref[:, at], kp_ref[:, at]), k_ref[:, at]], axis=0)
        values = jnp.concatenate([jnp.where(at_start, halo_ref[:, at_value], vp_ref[:, at]), v_ref[:, at]], axis=0)
        probs = probabilities(q_ref[:, at], keys, mask)
        out_ref[:, at] = matmul(probs.astype(low), values).astype(low)


def block_gradients(query, keys, values, mask, grad_mixed):
    probs = probabilities(query, keys, mask)
    grad_probs = matmul_right_t(grad_mixed, values)
    inner = jnp.sum(probs * grad_probs, axis=-1, keepdims=True)
    return (probs * (grad_probs - inner)).astype(low), probs.astype(low)


def halo_back_kernel(place, q_ref, k_ref, v_ref, halo_ref, mask_ref, gm_ref, back_ref):
    wide = q_ref.shape[1]
    for head in range(wide // HEAD):
        at = slice(head * HEAD, (head + 1) * HEAD)
        at_value = slice(wide + head * HEAD, wide + (head + 1) * HEAD)
        keys = jnp.concatenate([halo_ref[:, at], k_ref[:, at]], axis=0)
        values = jnp.concatenate([halo_ref[:, at_value], v_ref[:, at]], axis=0)
        grad_scores, probs = block_gradients(q_ref[:, at], keys, values, mask_ref[0], gm_ref[:, at])
        back_ref[:, at] = (matmul_left_t(grad_scores, q_ref[:, at])[:WIN] * SCALE).astype(low)
        back_ref[:, at_value] = matmul_left_t(probs, gm_ref[:, at])[:WIN].astype(low)


def halo_back(place, qkv, halo, mask, grad_mixed):
    wide = qkv.shape[1] // 3
    block = lambda column: pl.BlockSpec((BLOCK, wide), lambda s, place: (place[0], column))
    once = pl.BlockSpec((WIN, 2 * wide), lambda s, place: (0, 0))
    return pl.pallas_call(
        halo_back_kernel,
        grid_spec=pltpu.PrefetchScalarGridSpec(
            num_scalar_prefetch=1,
            grid=(1,),
            in_specs=[block(0), block(1), block(2), once]
            + [pl.BlockSpec((1, BLOCK, BLOCK + WIN), lambda s, place: (place[0], 0, 0)), block(0)],
            out_specs=once,
        ),
        out_shape=jax.ShapeDtypeStruct((WIN, 2 * wide), low),
        compiler_params=pltpu.CompilerParams(vmem_limit_bytes=8 << 20),
        cost_estimate=FILLS,
    )(place, qkv, qkv, qkv, halo, mask, grad_mixed)


def attend_back_kernel(
    place, q_ref, k_ref, v_ref, kp_ref, vp_ref, halo_ref, mask_ref, gm_ref, grads_ref, tail_ref, carry
):
    step = pl.program_id(0)
    mask = mask_ref[0]
    wide = q_ref.shape[1]
    at_start = step == N_TEAM - 1

    @pl.when(step == 0)
    def _():
        carry[...] = jnp.zeros_like(carry)

    for head in range(wide // HEAD):
        at = slice(head * HEAD, (head + 1) * HEAD)
        at_value = slice(wide + head * HEAD, wide + (head + 1) * HEAD)
        query = q_ref[:, at]
        keys = jnp.concatenate([jnp.where(at_start, halo_ref[:, at], kp_ref[:, at]), k_ref[:, at]], axis=0)
        values = jnp.concatenate([jnp.where(at_start, halo_ref[:, at_value], vp_ref[:, at]), v_ref[:, at]], axis=0)
        grad_mixed = gm_ref[:, at]
        grad_scores, probs = block_gradients(query, keys, values, mask, grad_mixed)
        grads_ref[:, at] = (matmul(grad_scores, keys) * SCALE).astype(low)
        grad_keys = matmul_left_t(grad_scores, query) * SCALE
        grad_values = matmul_left_t(probs, grad_mixed)
        for here, grad in ((at, grad_keys), (at_value, grad_values)):
            there = slice(wide + here.start, wide + here.stop)
            last = grad[BLOCK:] + carry[:, here]
            grads_ref[: BLOCK - WIN, there] = grad[WIN:BLOCK].astype(low)
            grads_ref[BLOCK - WIN :, there] = last.astype(low)

            @pl.when(step == 0)
            def _(last=last, here=here):
                tail_ref[:, here] = last

            carry[:, here] = grad[:WIN]


def attention_specs(wide, step):
    def block(rows, column, first):
        return pl.BlockSpec((rows, wide), lambda s, place: (place[first + step(s)], column))

    return [
        block(BLOCK, 0, 0),
        block(BLOCK, 1, 0),
        block(BLOCK, 2, 0),
        block(WIN, 1, N_TEAM),
        block(WIN, 2, N_TEAM),
        pl.BlockSpec((WIN, 2 * wide), lambda s, place: (0, 0)),
        pl.BlockSpec((1, BLOCK, BLOCK + WIN), lambda s, place: (place[step(s)], 0, 0)),
    ]


def attend(place, qkv, halo, mask):
    wide = qkv.shape[1] // 3
    return pl.pallas_call(
        attend_kernel,
        grid_spec=pltpu.PrefetchScalarGridSpec(
            num_scalar_prefetch=1,
            grid=(N_TEAM,),
            in_specs=attention_specs(wide, lambda s: s),
            out_specs=pl.BlockSpec((BLOCK, wide), lambda s, place: (place[s], 0)),
        ),
        out_shape=jax.ShapeDtypeStruct((N_TEAM * BLOCK, wide), low),
        compiler_params=pltpu.CompilerParams(vmem_limit_bytes=8 << 20),
        cost_estimate=FILLS,
    )(place, qkv, qkv, qkv, qkv, qkv, halo, mask)


def attend_back(place, qkv, halo, mask, grad_mixed):
    wide = qkv.shape[1] // 3
    step = lambda s: N_TEAM - 1 - s
    by_block = lambda width: pl.BlockSpec((BLOCK, width), lambda s, place: (place[step(s)], 0))
    once = pl.BlockSpec((WIN, 2 * wide), lambda s, place: (0, 0))
    return pl.pallas_call(
        attend_back_kernel,
        grid_spec=pltpu.PrefetchScalarGridSpec(
            num_scalar_prefetch=1,
            grid=(N_TEAM,),
            in_specs=attention_specs(wide, step) + [by_block(wide)],
            out_specs=[by_block(3 * wide), once],
            scratch_shapes=[pltpu.VMEM((WIN, 2 * wide), full)],
        ),
        out_shape=[
            jax.ShapeDtypeStruct((N_TEAM * BLOCK, 3 * wide), low),
            jax.ShapeDtypeStruct((WIN, 2 * wide), full),
        ],
        compiler_params=pltpu.CompilerParams(vmem_limit_bytes=8 << 20),
        cost_estimate=FILLS,
    )(place, qkv, qkv, qkv, qkv, qkv, halo, mask, grad_mixed)


def attn_terms_kernel(normed_ref, grad_ref, mixed_ref, hidden0_ref, hidden1_ref, out_ref, out_term):
    step = pl.program_id(0)
    half = hidden0_ref.shape[0]
    wide, deep = mixed_ref.shape[1], grad_ref.shape[1]
    rows = wide // N_FLEET

    @pl.when(step == 0)
    def _():
        out_term[...] = (
            matmul_left_t(mixed_ref[:half], hidden0_ref[...]) + matmul_left_t(mixed_ref[half:], hidden1_ref[...])
        ).astype(low)

    out_ref[:, :deep] = matmul_left_t(normed_ref[...], grad_ref[...]).astype(low)
    part = out_term[pl.ds(pl.multiple_of(step * rows, 32), rows)]
    for t in range(N_TEAM):
        out_ref[rows * t : rows * (t + 1), deep:] = part[:, wide * t : wide * (t + 1)]


def attn_terms(normed, grad_qkv, mixed, hidden_low):
    rows, width = normed.shape
    half, wide, deep = rows // 2, mixed.shape[1], grad_qkv.shape[1]
    block = width // N_FLEET
    whole = lambda shape: pl.BlockSpec(shape, lambda s: (0, 0))
    return pl.pallas_call(
        attn_terms_kernel,
        grid=(N_FLEET,),
        in_specs=[pl.BlockSpec((rows, block), lambda s: (0, s)), whole((rows, deep)), whole((rows, wide))]
        + [whole((half, width))] * 2,
        out_specs=pl.BlockSpec((block, deep + wide), lambda s: (s, 0)),
        out_shape=pltpu.HBM((width, deep + wide), low),
        scratch_shapes=[pltpu.VMEM((wide, width), low)],
        compiler_params=pltpu.CompilerParams(vmem_limit_bytes=18 << 20),
        cost_estimate=FILLS,
    )(normed, grad_qkv, mixed, *hidden_low)


def summed(refs, at):
    return refs[0][at] + sum(ref[at].astype(full) for ref in refs[1:])


def own_rows(kernel, out_types, *operands):
    shape = operands[0].shape
    n = len(operands)

    def whole(*refs):
        sources, outs, held, arrived = refs[:n], refs[n:-n - 1], refs[-n - 1 : -1], refs[-1]
        copies = [pltpu.make_async_copy(sources[i], held[i], arrived.at[i]) for i in range(n)]
        for copy in copies:
            copy.start()
        for copy in copies:
            copy.wait()
        for first in range(0, shape[0], 16):
            kernel(slice(first, first + 16), (*held, *outs))

    return pl.pallas_call(
        whole,
        in_specs=[pl.BlockSpec(memory_space=pl.ANY)] * n,
        out_shape=[jax.ShapeDtypeStruct(shape, dtype) for dtype in out_types],
        scratch_shapes=[pltpu.VMEM(operand.shape, operand.dtype) for operand in operands]
        + [pltpu.SemaphoreType.DMA((n,))],
        compiler_params=pltpu.CompilerParams(vmem_limit_bytes=12 << 20),
        cost_estimate=FILLS,
    )(*operands)


def hidden_kernel(at, refs):
    *parts, x_ref, gain_ref, hidden_ref, again_ref = refs
    hidden = x_ref[at].astype(full) + summed(parts, at)
    hidden_ref[at] = hidden
    again_ref[at] = (hidden * inverse_rms(hidden) * gain_ref[...]).astype(low)


def norm_backward(grad_normed, inputs, gain):
    scale_rows = inverse_rms(inputs)
    weighted = grad_normed * gain
    return scale_rows * weighted - inputs * scale_rows**3 * jnp.mean(
        weighted * inputs, axis=-1, keepdims=True
    )


def grad_hidden_kernel(at, refs):
    *parts, hidden_ref, dy_ref, gain_ref, grad_ref, low_ref = refs
    grad = dy_ref[at].astype(full) + norm_backward(summed(parts, at), hidden_ref[at], gain_ref[...])
    grad_ref[at] = grad
    low_ref[at] = grad.astype(low)


def input_grad_kernel(at, refs):
    *parts, x_ref, grad_ref, gain_ref, out_ref = refs
    out_ref[at] = grad_ref[at] + norm_backward(summed(parts, at), x_ref[at].astype(full), gain_ref[...])


def outputs_kernel(at, refs):
    *parts, hidden_ref, out_ref = refs
    out_ref[at] = (hidden_ref[at] + summed(parts, at)).astype(low)


def feed_owner_kernel(unit_rows, group, here_ref, there_ref, w_gate_ref, w_up_ref, gain_ref, gate_ref, up_ref, grad_ref):
    rows = here_ref.shape[1]
    units = here_ref.shape[2] // 2
    pad = units // N_FLEET
    first = group[0] == 0
    for t in range(N_TEAM):
        here, there = here_ref[t], there_ref[t]
        block = jnp.concatenate([jnp.where(first, here, there), jnp.where(first, there, here)], axis=0).astype(full)
        for i, out_ref in enumerate((gate_ref, up_ref)):
            for f in range(N_FLEET):
                at = i * units + f * pad
                to = (f * N_TEAM + t) * unit_rows
                out_ref[:, to : to + unit_rows] = block[:, at : at + unit_rows]
    for row in range(0, 2 * rows, 16):
        at = slice(row, row + 16)
        total = w_gate_ref[at].astype(full) * gate_ref[at] + w_up_ref[at].astype(full) * up_ref[at]
        grad_ref[at] = jnp.sum(total, axis=1, keepdims=True) / gain_ref[at].astype(full)


def feed_owner(group, here, there, w_gate, w_up, gain):
    shard, wide = w_gate.shape
    vmem = pl.BlockSpec(memory_space=pltpu.VMEM)
    return pl.pallas_call(
        functools.partial(feed_owner_kernel, wide // (N_FLEET * N_TEAM)),
        in_specs=[pl.BlockSpec(memory_space=pltpu.SMEM)] + [vmem] * 5,
        out_specs=[vmem] * 3,
        out_shape=[jax.ShapeDtypeStruct((shard, wide), full)] * 2 + [jax.ShapeDtypeStruct((shard, 1), full)],
        compiler_params=pltpu.CompilerParams(vmem_limit_bytes=10 << 20),
        cost_estimate=FILLS,
    )(group, here, there, w_gate, w_up, gain[:, None])


def attn_owner_kernel(
    sums_ref, out0_ref, out1_ref, w_query_ref, w_key_ref, w_value_ref, gain_ref,
    query_ref, key_ref, value_ref, out_ref, grad_ref,
):
    wide = sums_ref.shape[2] // 3
    weights = (w_query_ref, w_key_ref, w_value_ref)
    total = jnp.zeros((query_ref.shape[0], wide), full)
    for t in range(N_TEAM):
        to = slice(t * wide, (t + 1) * wide)
        block = sums_ref[t].astype(full) + sums_ref[N_TEAM + t].astype(full)
        for i, grad in enumerate((query_ref, key_ref, value_ref)):
            part = block[:, i * wide : (i + 1) * wide]
            grad[:, to] = part
            total += part * weights[i][:, to].astype(full)
        out_ref[:, to] = out0_ref[t].astype(full) + out1_ref[t].astype(full)
    grad_ref[...] = jnp.sum(total, axis=1, keepdims=True) / gain_ref[...].astype(full)


def attn_owner(sums, out_sums, w_query, w_key, w_value, gain):
    grad = jax.ShapeDtypeStruct(w_query.shape, full)
    return pl.pallas_call(
        attn_owner_kernel,
        out_shape=[grad] * 4 + [jax.ShapeDtypeStruct((w_query.shape[0], 1), full)],
        compiler_params=pltpu.CompilerParams(vmem_limit_bytes=8 << 20),
        cost_estimate=FILLS,
    )(sums, *out_sums, w_query, w_key, w_value, gain[:, None])


def body(
    tokens, lengths, norm_gain, w_query, w_key, w_value, w_out, mlp_gain, w_gate, w_up, w_down, cotangent
):
    rows, width = tokens.shape
    shard = w_query.shape[0]
    team_wide = width // N_TEAM
    unit_rows = w_down.shape[0]
    unit_pad = -(-unit_rows // 32) * 32
    units = N_FLEET * unit_pad
    x, yl, z, c = [lax.axis_index(axis) for axis in ("x", "yl", "z", "c")]
    fleet = lax.axis_index(FLEET)

    order = jnp.arange(N_TEAM, dtype=jnp.int32)
    spot = (jnp.bitwise_xor(order % N_C, c) * N_Z + (order // N_C - z) % N_Z).astype(jnp.int32)
    before = jnp.concatenate([jnp.zeros((1,), jnp.int32), 2 * spot[:-1] + 1])
    place = jnp.concatenate([spot, before])
    last_spot = (1 - c) * N_Z + N_Z - 1 - z
    last_at = last_spot * BLOCK + BLOCK - WIN
    kept = jnp.arange(N_TEAM, dtype=jnp.int32)
    kept_block = N_C * ((kept % N_Z + z) % N_Z) + jnp.bitwise_xor(kept // N_Z, c)
    first_pos = (fleet * N_TEAM + kept_block) * BLOCK
    query_pos = first_pos[:, None] + jnp.arange(BLOCK, dtype=jnp.int32)
    key_pos = first_pos[:, None] - WIN + jnp.arange(BLOCK + WIN, dtype=jnp.int32)
    query_segs = segment_numbers(query_pos, lengths[0])
    key_segs = jnp.where(key_pos >= 0, segment_numbers(key_pos, lengths[0]), -1)
    distance = query_pos[:, :, None] - key_pos[:, None, :]
    mask = (distance >= 0) & (distance < WIN) & (query_segs[:, :, None] == key_segs[:, None, :])
    mask = mask.astype(full)

    out_there = swapped(w_out)
    x_mine = [tokens, from_ahead(tokens, "z", 1), None, from_ahead(tokens, "z", 3)]
    cut = attn_cut(w_query, w_key, w_value, norm_gain, mlp_gain)
    cut = lax.all_to_all(cut, TEAM, 0, 0, tiled=True).reshape(N_TEAM * shard, -1)
    out_cut = out_there.reshape(shard, N_TEAM, team_wide).transpose(1, 0, 2)
    out_cut = out_cut.reshape(N_TEAM * shard, team_wide)
    cut, out_cut, x_mine, w_gate_later, dy = lax.optimization_barrier((cut, out_cut, x_mine, w_gate, cotangent))
    qkv_piece, rest = cut[:, : 3 * team_wide], jnp.concatenate([cut[:, 3 * team_wide :], out_cut], axis=1)
    along_y = lambda value, by: from_ahead(value, ("g", "yl"), by)
    other = lambda block: from_ahead(block, "c", 1)
    attn = lax.all_to_all(jnp.broadcast_to(qkv_piece, (N_X, *qkv_piece.shape)), "x", 0, 0, tiled=True)
    attn = attn.reshape(width // 2, -1)
    half_rest = rest.shape[0] // 2
    rest_there = along_y(rest[:half_rest], 1), along_y(rest[half_rest:], -1)
    x_mine[2] = from_ahead(x_mine[0], "z", 2)
    x_other = [other(x_mine[0]), other(x_mine[1]), None, other(x_mine[3])]
    gate_up = feed_cut(w_gate_later, w_up, unit_rows, units)
    down_piece = pack(w_down, unit_pad, 2 * units)
    attn, rest_there, x_mine, x_other, dy, gate_up, down_piece, place, mask = lax.optimization_barrier(
        (attn, rest_there, x_mine, x_other, dy, gate_up, down_piece, place, mask)
    )
    pair = jnp.concatenate([rest, *rest_there], axis=0)
    pairs = [pair] + [from_ahead(pair, "x", k) for k in (1, 2, 3)]
    x_other[2] = other(x_mine[2])
    gate_up_piece = lax.all_to_all(gate_up, TEAM, 0, 0, tiled=True).reshape(N_TEAM * shard, -1)
    attn_there = along_y(attn[: width // 4], 1), along_y(attn[width // 4 :], -1)
    attn, attn_there, pairs, x_mine, x_other, dy, gate_up_piece = lax.optimization_barrier(
        (attn, attn_there, pairs, x_mine, x_other, dy, gate_up_piece)
    )
    dy_mine = z_gather(dy)
    x_blocks = x_mine + x_other
    halo = along_line(lax.select_n(last_spot, *[block[BLOCK - WIN :] for block in x_blocks]), 1)
    feed_piece = jnp.concatenate([gate_up_piece, down_piece], axis=0)
    w_feed = lax.all_gather(feed_piece, FLEET, axis=0, tiled=False)

    half = N_Z * BLOCK
    w_qkv, w_out_team, gain_rows = assemble(jnp.stack([yl, x]).astype(jnp.int32), attn, attn_there, pairs)
    normed = normalised(x_blocks, gain_rows)
    gain_one, gain_two = gain_rows[:1], gain_rows[1:2]
    qkv = matmul(normed, w_qkv).astype(low)
    qkv, halo = lax.optimization_barrier((qkv, halo))
    halo = halo.astype(full)
    halo = matmul((halo * inverse_rms(halo) * gain_one).astype(low), w_qkv[:, team_wide:]).astype(low)
    mixed = attend(place, qkv, halo, mask)
    halves = lambda rows: (rows[:half], rows[half : 2 * half])
    hidden_blocks = core_sum(halves(mixed), lambda rows: matmul(rows, w_out_team))
    hidden_blocks, dy_mine = lax.optimization_barrier((hidden_blocks, dy_mine))
    dy_other = [other(block) for block in dy_mine]
    hidden_parts, dy_mine, dy_other = lax.optimization_barrier((z_send(hidden_blocks), dy_mine, dy_other))

    hidden, again = own_rows(hidden_kernel, (full, low), *hidden_parts, tokens, gain_two)
    again = z_gather(again)
    again_other = [other(block) for block in again[:2]] + [None, other(again[3])]
    again, again_other[:2], again_other[3] = lax.optimization_barrier((again, again_other[:2], again_other[3]))
    again_other[2] = other(again[2])
    w_gate_up, w_down_team = unpack(w_feed, N_TEAM * shard, unit_pad, width)
    act_mine, gate_mine, up_mine, x_mine, dy_mine = feed(again, dy_mine, w_gate_up, w_down_team)
    act_other, gate_other, up_other, x_other, dy_other = feed(again_other, dy_other, w_gate_up, w_down_team)
    there = feed_back(gate_other, up_other, w_gate_up, low)
    again_blocks = core_blocks(feed_back(gate_mine, up_mine, w_gate_up, full), there)
    activated, grad_gate, grad_up = (act_mine, act_other), (gate_mine, gate_other), (up_mine, up_other)
    again_blocks, activated, grad_gate, grad_up = lax.optimization_barrier(
        (again_blocks, activated, grad_gate, grad_up)
    )
    mlp_term = feed_terms((x_mine, x_other), (dy_mine, dy_other), activated, grad_gate, grad_up)
    again_parts = z_send(again_blocks)
    mlp_term, again_parts[1], again_parts[3] = lax.optimization_barrier((mlp_term, again_parts[1], again_parts[3]))
    mlp_sum = lax.psum_scatter(
        mlp_term.reshape(-1, 2 * units), ("g", *FLEET), scatter_dimension=0, tiled=True
    )

    grad_hidden, hidden_low = own_rows(grad_hidden_kernel, (full, low), *again_parts, hidden, cotangent, gain_two)
    output_parts = down_parts(activated, w_down_team)
    hidden_low, output_parts = lax.optimization_barrier((z_gather(hidden_low), output_parts))
    hidden_low = [join(hidden_low)]
    hidden_low.append(other(hidden_low[0]))
    output_blocks = core_blocks(*output_parts)

    grad_mixed = [matmul_right_t(rows, w_out_team).astype(low) for rows in hidden_low]
    grad_mixed = jnp.concatenate(grad_mixed, axis=0)
    back = halo_back(place, qkv, halo, mask, grad_mixed)
    grad_qkv, tail = attend_back(place, qkv, halo, mask, grad_mixed)
    tail = tail + along_line(back, -1).astype(full)
    grad_qkv = lax.dynamic_update_slice(grad_qkv, tail.astype(low), (last_at, team_wide))
    attn_term = attn_terms(normed, grad_qkv, mixed, hidden_low)
    attn_term, grad_qkv, output_parts = lax.optimization_barrier((attn_term, grad_qkv, z_send(output_blocks)))
    attn_sum = lax.psum_scatter(attn_term, FLEET, scatter_dimension=0, tiled=True)
    (outputs,) = own_rows(outputs_kernel, (low,), *output_parts, hidden)
    normed_blocks = core_sum(halves(grad_qkv), lambda rows: matmul_right_t(rows, w_qkv))

    down_sum = unpack_down(mlp_sum[N_TEAM * shard // 2 :], unit_pad // 2, width)
    gate_up_sum = mlp_sum[: N_TEAM * shard // 2].reshape(N_TEAM, shard // 2, 2 * units)
    gate_up_sum = lax.all_to_all(gate_up_sum, TEAM, 0, 0, tiled=True)
    normed_blocks, gate_up_sum, down_sum = lax.optimization_barrier((normed_blocks, gate_up_sum, down_sum))
    gate_up_there, down_there = from_ahead(gate_up_sum, "g", 1), from_ahead(down_sum, "g", 1)
    normed_parts, attn_sum, outputs, gate_up_there, down_there = lax.optimization_barrier(
        (z_send(normed_blocks), attn_sum, outputs, gate_up_there, down_there)
    )
    (input_grad,) = own_rows(input_grad_kernel, (full,), *normed_parts, tokens, grad_hidden, gain_one)
    qkv_sum = attn_sum[:, : 3 * team_wide].reshape(N_TEAM, shard, 3 * team_wide)
    qkv_sum = lax.all_to_all(jnp.concatenate([qkv_sum, qkv_sum], axis=0), ("g", *TEAM), 0, 0, tiled=True)
    out_sum = attn_sum[:, 3 * team_wide :].reshape(N_TEAM, shard, team_wide)
    group = lax.axis_index("g")
    gate_grad, up_grad, mlp_gain_grad = feed_owner(
        group[None].astype(jnp.int32), gate_up_sum, gate_up_there, w_gate, w_up, mlp_gain
    )
    qkv_sum, out_sums, input_grad, gate_grad = lax.optimization_barrier(
        (qkv_sum, (swapped(out_sum), swapped(out_sum, 1)), input_grad, gate_grad)
    )
    query_grad, key_grad, value_grad, out_grad, gain_grad = attn_owner(
        qkv_sum, out_sums, w_query, w_key, w_value, norm_gain
    )
    first, second = jnp.where(group == 0, down_sum, down_there), jnp.where(group == 0, down_there, down_sum)
    down_grad = jnp.concatenate([first, second], axis=0)[:unit_rows].astype(full)
    return (
        outputs,
        input_grad,
        gain_grad[:, 0],
        query_grad,
        key_grad,
        value_grad,
        out_grad,
        mlp_gain_grad[:, 0],
        gate_grad,
        up_grad,
        down_grad,
    )


def solution(mesh):
    fine = Mesh(mesh.devices.reshape(2, 2, 4, 4, 2), ALL)
    return jax.shard_map(
        body,
        mesh=fine,
        in_specs=(
            P(ALL, None),
            P("g", None),
            P(SEQ),
            P(SEQ, None),
            P(SEQ, None),
            P(SEQ, None),
            P(SEQ, None),
            P(SEQ),
            P(SEQ, None),
            P(SEQ, None),
            P(SEQ, None),
            P(ALL, None),
        ),
        out_specs=(
            P(ALL, None),
            P(ALL, None),
            P(SEQ),
            P(SEQ, None),
            P(SEQ, None),
            P(SEQ, None),
            P(SEQ, None),
            P(SEQ),
            P(SEQ, None),
            P(SEQ, None),
            P(SEQ, None),
        ),
        check_vma=False,
    )
```
